512 devices in a mesh: group: 16 (over z_hi, y), tensor: 32 (over x, z_lo, core).
Axes of the slice: x: 4, y: 4, z: 16 (z_hi: 4, z_lo: 4; z = z_hi * 4 + z_lo), core: 2. Of those that a mesh axis runs over, the one named last changes fastest.
Arguments:
- step_inputs: bfloat16 [4, 512, 4096], P(None, 'group', 'tensor'), may hold values from -6 to 6
- qkv_weight: bfloat16 [4096, 3, 4096], P(None, None, 'tensor'), may hold values from -0.09375 to 0.09375
- out_weight: bfloat16 [4096, 4096], P('tensor'), may hold values from -0.09375 to 0.09375
- head_gain: float32 [4096], P('tensor'), may hold values from 0.1 to 1.9
- head_decay: float32 [32], P('tensor'), may hold values from 0.3 to 0.98
- states_in: float32 [512, 32, 128, 128], P('group', 'tensor'), may hold values from -3 to 3
- remaining_steps: int32 [512], replicated, may hold values from 0 to 8, as said below
- migration_plan: int32 [512], replicated, may hold values from 0 to 511, as said below
Outputs:
- step_outputs: bfloat16 [4, 512, 4096], P(None, 'group', 'tensor')
The draws below stay inside these ranges and needn't reach their ends.
Inputs may be any that keep to these rules, and one draw needn't show every extreme that they name: A permutation: row j after the move holds the sequence that row migration_plan[j] held. In each group exactly 13 rows receive a sequence from another group and exactly 13 rows send one to another group, at most 2 between any two groups, and 2 from one of them; all other rows keep their own sequence. `remaining_steps`: A sequence that the plan moves to another group has 4 or more steps left.
All inputs are finite; a program needn't handle non-finite values.
Results may differ from the reference program's by a relative error of at most 0.0065.
Values may be sent and summed in bfloat16 or wider, within the bound.
No kernel may reach another device: no remote copies, remote signals or barrier semaphores. Data moves between devices by JAX's collectives and lax.ppermute only.
A program may use at most 128 MiB of HBM per device.

```python
import jax
import jax.numpy as jnp
from jax import lax

D = 4096
HD = 128
HEADS = 32
BATCH = 32
STEPS = 4
MOVE = 13
GROUPS = 16
ROWS = 512


def migration_helper(key):
    key = jax.random.fold_in(key, 11)
    shift_key, order_key = jax.random.split(key)
    shift_order = jax.random.permutation(shift_key, GROUPS - 1) + 1
    round_shift = jnp.concatenate([shift_order[:1], shift_order[:MOVE - 1]])
    orders = jax.vmap(lambda sub_key: jax.random.permutation(sub_key, BATCH))(jax.random.split(order_key, GROUPS))
    group_ids = jnp.arange(GROUPS)
    dest_slots = []
    source_slots = []
    for round_index in range(MOVE):
        source_ids = (group_ids - round_shift[round_index]) % GROUPS
        dest_slots.append(group_ids * BATCH + orders[:, round_index])
        source_slots.append(source_ids * BATCH + orders[source_ids, round_index])
    slot_plan = jnp.arange(ROWS).at[jnp.concatenate(dest_slots)].set(jnp.concatenate(source_slots))
    return (slot_plan.astype(jnp.int32), orders)


def draw_migration_plan(key, part):
    slot_plan, orders = migration_helper(key)
    return slot_plan


def draw_remaining_steps(key, part):
    slot_plan, orders = migration_helper(key)
    key = jax.random.fold_in(key, 3)
    draw_steps = jax.random.randint(key, (ROWS,), 0, 2 * STEPS + 1)
    group_ids = jnp.arange(GROUPS)
    moved_slots = (group_ids[:, None] * BATCH + orders[:, :MOVE]).reshape(-1)
    draw_steps = draw_steps.at[moved_slots].set(jnp.maximum(draw_steps[moved_slots], STEPS))
    draw_steps = draw_steps.at[orders[0, 0]].set(2 * STEPS)
    draw_steps = draw_steps.at[orders[0, BATCH - 1]].set(0)
    return draw_steps.astype(jnp.int32)


def steps_of(own_key, extent, cuts, low, high):
    def one(dim, shards_of):
        heights = jax.random.uniform(jax.random.fold_in(jax.random.fold_in(own_key, 6), dim), (shards_of,), jnp.float32, low / len(cuts), high / len(cuts))
        return jnp.repeat(jnp.exp(heights), extent[dim] // shards_of).reshape((-1,) + (1,) * (len(extent) - dim - 1))

    level = one(*cuts[0])
    for cut in cuts[1:]:
        level = level * one(*cut)
    return level


def bell_draw(rng, shape, deviation, reach, cuts=(), kind=jnp.bfloat16):
    drawn = deviation * jax.random.normal(rng, shape, jnp.float32)
    if cuts:
        drawn = drawn * steps_of(rng, shape, cuts, -0.22, 0.18)
    return jnp.clip(drawn, -reach, reach).astype(kind)


def setup_inputs(seed: int = 0) -> dict:
    keys = jax.random.split(jax.random.key(seed), 9)
    return {
        "step_inputs": bell_draw(keys[0], (STEPS, ROWS, D), 1.0, 6.0, ((1, 16), (2, 32))),
        "qkv_weight": bell_draw(keys[1], (D, 3, HEADS * HD), D ** -0.5, 0.09375, ((2, 32),)),
        "out_weight": bell_draw(keys[2], (HEADS * HD, D), (HEADS * HD) ** -0.5, 0.09375, ((0, 32),)),
        "head_gain": jnp.clip(1.0 + 0.18 * jax.random.normal(keys[3], (HEADS * HD,), jnp.float32), 0.1, 1.9),
        "head_decay": jnp.clip(0.3 + 0.68 * jax.random.uniform(keys[4], (HEADS,), jnp.float32) ** steps_of(keys[4], (HEADS,), ((0, 32),), -0.2, 0.2), 0.3, 0.98),
        "states_in": bell_draw(keys[5], (ROWS, HEADS, HD, HD), 0.5, 3.0, ((0, 16), (1, 32)), jnp.float32),
        "remaining_steps": draw_remaining_steps(jax.random.fold_in(keys[8], 71), 0),
        "migration_plan": draw_migration_plan(jax.random.fold_in(keys[8], 71), 0),
    }


def reference(step_inputs, qkv_weight, out_weight, head_gain, head_decay, states_in, remaining_steps, migration_plan):
    states = jnp.take(states_in, migration_plan, axis=0)
    steps_left = jnp.take(remaining_steps, migration_plan, axis=0)
    proj_weight = qkv_weight.reshape(D, 3 * HEADS * HD)
    gain_rows = head_gain.reshape(HEADS, HD)
    outputs = []
    for step_index in range(STEPS):
        projected = jnp.dot(step_inputs[step_index], proj_weight, preferred_element_type=jnp.float32)
        projected = projected.reshape(ROWS, 3, HEADS, HD)
        query_vec = jax.nn.silu(projected[:, 0])
        key_vec = jax.nn.silu(projected[:, 1])
        value_vec = projected[:, 2]
        active = steps_left > step_index
        updated = head_decay[None, :, None, None] * states + key_vec[:, :, :, None] * value_vec[:, :, None, :]
        states = jnp.where(active[:, None, None, None], updated, states)
        readout = jnp.einsum('bhd,bhde->bhe', query_vec, states, precision=lax.Precision.HIGHEST)
        scale_inv = lax.rsqrt(lax.optimization_barrier(jnp.mean(readout * readout, axis=-1, keepdims=True)) + 1e-05)
        normed = readout * scale_inv * gain_rows[None]
        normed = jnp.where(active[:, None, None], normed, jnp.zeros_like(normed))
        normed = normed.astype(jnp.bfloat16).reshape(ROWS, HEADS * HD)
        outputs.append(jnp.dot(normed, out_weight, preferred_element_type=jnp.float32).astype(jnp.bfloat16))
    return jnp.stack(outputs)
```

```python
import jax
import jax.numpy as jnp
from jax import lax
from jax.sharding import PartitionSpec as P

STEPS = 4
XS, ZS, CORES = 4, 4, 2
SLOTS = 2


def tensor_id(x, z, c):
    return (x * ZS + z) * CORES + c


Z_LINES = [[tensor_id(x, z, c) for z in range(ZS)] for x in range(XS) for c in range(CORES)]
X_RINGS = [[tensor_id(x, z, c) for x in range(XS)] for z in range(ZS) for c in range(CORES)]
CORE_SWAP = [
    (tensor_id(x, z, c), tensor_id(x, z, 1 - c))
    for x in range(XS)
    for z in range(ZS)
    for c in range(CORES)
]


def ranks(same):
    rows = same.shape[-1]
    earlier = jnp.arange(rows)[None, :] < jnp.arange(rows)[:, None]
    return jnp.sum((same & earlier).astype(jnp.int32), axis=-1)


def move_states(states, migration_plan, own_group, groups):
    rows = states.shape[0]
    plan = migration_plan.reshape(groups, rows)
    source_group, source_slot = plan // rows, plan % rows
    from_here = source_group == own_group
    order = ranks(jnp.broadcast_to(from_here[:, None, :], (groups, rows, rows)))
    wanted = from_here[:, None, :] & (order[:, None, :] == jnp.arange(SLOTS)[None, :, None])
    chosen = jnp.sum(jnp.where(wanted, source_slot[:, None, :], 0), axis=-1)
    outgoing = jnp.take(states, chosen.reshape(-1), axis=0).astype(jnp.bfloat16)
    outgoing = outgoing.reshape(groups, SLOTS, *states.shape[1:])
    incoming = lax.all_to_all(outgoing, "group", 0, 0, tiled=True)
    return incoming.reshape(groups * SLOTS, *states.shape[1:])


def gather_features(own, core):
    line = lax.all_gather(own, "tensor", axis=0, axis_index_groups=Z_LINES)
    plane = lax.all_gather(line, "tensor", axis=0, axis_index_groups=X_RINGS)
    other = lax.ppermute(plane, "tensor", CORE_SWAP)
    even = jnp.where(core == 0, plane, other)
    odd = jnp.where(core == 0, other, plane)
    whole = jnp.stack([even, odd], axis=2)
    return jnp.transpose(whole, (3, 0, 1, 2, 4)).reshape(own.shape[0], -1)


def scatter_sums(normed, out_weight, core):
    rows, depth = normed.shape
    split = out_weight.reshape(depth, XS * ZS, CORES, -1)

    def part(which):
        weight = lax.dynamic_index_in_dim(split, which, axis=2, keepdims=False)
        value = jnp.einsum("rd,dpk->prk", normed, weight, preferred_element_type=jnp.float32)
        return value

    received = lax.ppermute(part(1 - core).astype(jnp.bfloat16), "tensor", CORE_SWAP)
    plane = (part(core) + received.astype(jnp.float32)).astype(jnp.bfloat16)
    plane = plane.reshape(XS, ZS, rows, -1)
    pieces = lax.all_to_all(plane, "tensor", 0, 0, tiled=True, axis_index_groups=X_RINGS)
    line = jnp.sum(pieces.astype(jnp.float32), axis=0).astype(jnp.bfloat16)
    pieces = lax.all_to_all(line, "tensor", 0, 0, tiled=True, axis_index_groups=Z_LINES)
    return jnp.sum(pieces.astype(jnp.float32), axis=0).astype(jnp.bfloat16)


def body(
    step_inputs,
    qkv_weight,
    out_weight,
    head_gain,
    head_decay,
    states_in,
    remaining_steps,
    migration_plan,
):
    rows = states_in.shape[0]
    size = states_in.shape[2]
    groups = lax.axis_size("group")
    own_group = lax.axis_index("group")
    core = lax.axis_index("tensor") % CORES
    states_in = states_in.reshape(rows, size, size)

    incoming = move_states(states_in, migration_plan, own_group, groups)
    own_plan = lax.dynamic_slice_in_dim(migration_plan, own_group * rows, rows)
    source_group, source_slot = own_plan // rows, own_plan % rows
    arrival = source_group * SLOTS + ranks(source_group[:, None] == source_group[None, :])
    steps_left = jnp.take(remaining_steps, own_plan, axis=0)

    features = gather_features(step_inputs.reshape(STEPS * rows, -1), core)
    projected = jnp.dot(
        features, qkv_weight.reshape(qkv_weight.shape[0], -1), preferred_element_type=jnp.float32
    ).reshape(STEPS, rows, 3, size)
    query = jax.nn.silu(projected[:, :, 0])
    key = jax.nn.silu(projected[:, :, 1])
    value = projected[:, :, 2]

    kept = jnp.take(states_in, source_slot, axis=0)
    moved = jnp.take(incoming, jnp.clip(arrival, 0, groups * SLOTS - 1), axis=0)
    states = jnp.where(
        (source_group != own_group)[:, None, None], moved.astype(jnp.float32), kept
    )

    decay = head_decay[0]
    from_states = jnp.einsum("trd,rde->tre", query, states, precision=lax.Precision.HIGHEST)
    outs = []
    power = decay
    for t in range(STEPS):
        readout = power * from_states[t]
        power = power * decay
        weight = jnp.ones((), jnp.float32)
        for s in range(t, -1, -1):
            score = jnp.sum(query[t] * key[s], axis=-1, keepdims=True)
            readout = readout + (weight * score) * value[s]
            weight = weight * decay
        scale = lax.rsqrt(jnp.mean(readout * readout, axis=-1, keepdims=True) + 1e-05)
        normed = readout * scale * head_gain[None]
        outs.append(jnp.where((steps_left > t)[:, None], normed, 0.0))
    normed = jnp.stack(outs).astype(jnp.bfloat16).reshape(STEPS * rows, size)
    result = scatter_sums(normed, out_weight, core)
    return result.reshape(STEPS, rows, size)


def solution(mesh):
    placed = (
        P(None, "group", "tensor"),
        P(None, None, "tensor"),
        P("tensor", None),
        P("tensor"),
        P("tensor"),
        P("group", "tensor", None, None),
        P(),
        P(),
    )
    return jax.shard_map(
        body, mesh=mesh, in_specs=placed, out_specs=P(None, "group", "tensor"), check_vma=False
    )
```

```python
import functools

import jax
import jax.numpy as jnp
from jax import lax
from jax.experimental import pallas as pl
from jax.experimental.pallas import tpu as pltpu
from jax.sharding import PartitionSpec as P

STEPS = 4
SIZE = 128
MOVED = 13
XS, ZS, CORES = 4, 4, 2
CHIPS = XS * ZS
SLOTS = 2


def tensor_id(x, z, c):
    return (x * ZS + z) * CORES + c


Z_LINES = [[tensor_id(x, z, c) for z in range(ZS)] for x in range(XS) for c in range(CORES)]
X_RINGS = [[tensor_id(x, z, c) for x in range(XS)] for z in range(ZS) for c in range(CORES)]
CORE_SWAP = [
    (tensor_id(x, z, c), tensor_id(x, z, 1 - c))
    for x in range(XS)
    for z in range(ZS)
    for c in range(CORES)
]

VMEM = pl.BlockSpec(memory_space=pltpu.VMEM)
SMEM = pl.BlockSpec(memory_space=pltpu.SMEM)
ANY = pl.BlockSpec(memory_space=pl.ANY)


def ranks(same):
    rows = same.shape[-1]
    earlier = jnp.arange(rows)[None, :] < jnp.arange(rows)[:, None]
    return jnp.sum((same & earlier).astype(jnp.int32), axis=-1)


def after_kernel(x_ref, dep_ref, out_ref):
    pass


def after(x, dep):
    return pl.pallas_call(
        after_kernel,
        out_shape=jax.ShapeDtypeStruct(x.shape, x.dtype),
        in_specs=[ANY, ANY],
        out_specs=ANY,
        input_output_aliases={0: 0},
        name="after",
    )(x, dep)


def pack_states(states, migration_plan, own_group, groups):
    rows = states.shape[0]
    plan = migration_plan.reshape(groups, rows)
    source_group, source_slot = plan // rows, plan % rows
    from_here = source_group == own_group
    order = ranks(jnp.broadcast_to(from_here[:, None, :], (groups, rows, rows)))
    wanted = from_here[:, None, :] & (order[:, None, :] == jnp.arange(SLOTS)[None, :, None])
    chosen = jnp.sum(jnp.where(wanted, source_slot[:, None, :], 0), axis=-1)
    outgoing = jnp.take(states, chosen.reshape(-1), axis=0).astype(jnp.bfloat16)
    return outgoing.reshape(groups, SLOTS, *states.shape[1:])


def split_rows(q):
    high = q.astype(jnp.bfloat16)
    low = (q - high.astype(jnp.float32)).astype(jnp.bfloat16)
    return jnp.concatenate([high, low], axis=0)


def project_kernel(
    rows, where_ref, plan_ref, decay_ref, own_ref, other_ref, weight_ref, states_ref,
    query_ref, partial_ref, kept_ref,
):
    group, core = where_ref[0], where_ref[1]
    count = STEPS * rows
    acc = [jnp.zeros((count, SIZE), jnp.float32) for _ in range(3)]
    for chip in range(CHIPS):
        a, b = own_ref[chip], other_ref[chip]
        even = jnp.where(core == 0, a, b)
        odd = jnp.where(core == 0, b, a)
        both = jnp.concatenate([even, odd], axis=1)
        for i in range(3):
            weight = weight_ref[i, 2 * SIZE * chip : 2 * SIZE * (chip + 1), :]
            acc[i] += jnp.dot(both, weight, preferred_element_type=jnp.float32)
    query = acc[0] / (1.0 + jnp.exp(-acc[0]))
    key = acc[1] / (1.0 + jnp.exp(-acc[1]))
    value = acc[2]
    query_ref[...] = query
    for row in range(rows):
        source = plan_ref[group * rows + row]
        state = states_ref[source % rows]
        high = state.astype(jnp.bfloat16)
        low = (state - high.astype(jnp.float32)).astype(jnp.bfloat16)
        mine = query_ref[pl.ds(row, STEPS, stride=rows), :]
        pair = split_rows(mine)
        first = jnp.dot(pair, high, preferred_element_type=jnp.float32)
        second = jnp.dot(pair[:STEPS], low, preferred_element_type=jnp.float32)
        product = first[:STEPS] + first[STEPS:] + second
        stays = (source // rows == group).astype(jnp.float32)
        kept_ref[pl.ds(row, STEPS, stride=rows), :] = product * stays
    decay = decay_ref[0]
    at = lambda x, t: x[t * rows : (t + 1) * rows]
    power = decay
    for t in range(STEPS):
        readout = power * at(kept_ref, t)
        power = power * decay
        weight = jnp.float32(1.0)
        for s in range(t, -1, -1):
            score = jnp.sum(at(query, t) * at(key, s), axis=-1, keepdims=True)
            readout = readout + (weight * score) * at(value, s)
            weight = weight * decay
        partial_ref[t * rows : (t + 1) * rows] = readout


def finish_kernel(
    rows, where_ref, plan_ref, remaining_ref, decay_ref, query_ref, partial_ref, incoming_ref,
    gain_ref, weight_ref, own_ref, other_ref, readout_ref, active_ref, row_ref, slot_ref, seen_ref,
):
    group, core = where_ref[0], where_ref[1]
    groups = where_ref[2]
    decay = decay_ref[0]

    def clear(i, carry):
        seen_ref[i] = 0
        return carry

    lax.fori_loop(0, groups, clear, 0)
    for i in range(MOVED):
        row_ref[i] = 0
        slot_ref[i] = 0

    def scan(row, count):
        source = plan_ref[group * rows + row]
        source_group = source // rows
        rank = seen_ref[source_group]
        seen_ref[source_group] = rank + 1
        moved = source_group != group
        place = jnp.minimum(count, MOVED - 1)

        @pl.when(moved)
        def _():
            row_ref[place] = row
            slot_ref[place] = source_group * SLOTS + jnp.minimum(rank, SLOTS - 1)

        steps = remaining_ref[source]
        active_ref[pl.ds(row, 1), :] = jnp.full((1, SIZE), steps, jnp.int32)
        return count + moved.astype(jnp.int32)

    lax.fori_loop(0, rows, scan, 0)
    readout_ref[...] = partial_ref[...]
    power = lax.broadcasted_iota(jnp.int32, (STEPS, SIZE), 0)
    scale = jnp.where(power == 0, decay, 0.0)
    running = decay
    for t in range(1, STEPS):
        running = running * decay
        scale = jnp.where(power == t, running, scale)
    for i in range(MOVED):
        row = row_ref[i]
        mine = query_ref[pl.ds(row, STEPS, stride=rows), :]
        product = jnp.dot(
            split_rows(mine), incoming_ref[slot_ref[i]], preferred_element_type=jnp.float32
        )
        product = product[:STEPS] + product[STEPS:]
        readout_ref[pl.ds(row, STEPS, stride=rows), :] += scale * product
    pieces = []
    for t in range(STEPS):
        readout = readout_ref[t * rows : (t + 1) * rows]
        norm = lax.rsqrt(jnp.mean(readout * readout, axis=-1, keepdims=True) + 1e-05)
        normed = readout * norm * gain_ref[...]
        pieces.append(jnp.where(active_ref[...] > t, normed, 0.0))
    normed = jnp.concatenate(pieces, axis=0).astype(jnp.bfloat16)
    for chip in range(CHIPS):
        weight = weight_ref[:, 2 * SIZE * chip : 2 * SIZE * (chip + 1)]
        both = jnp.dot(normed, weight, preferred_element_type=jnp.float32)
        even, odd = both[:, :SIZE], both[:, SIZE:]
        own_ref[chip] = jnp.where(core == 0, even, odd)
        other_ref[chip] = jnp.where(core == 0, odd, even).astype(jnp.bfloat16)


def body(
    step_inputs,
    qkv_weight,
    out_weight,
    head_gain,
    head_decay,
    states_in,
    remaining_steps,
    migration_plan,
):
    rows = states_in.shape[0]
    count = STEPS * rows
    groups = lax.axis_size("group")
    own_group = lax.axis_index("group")
    core = lax.axis_index("tensor") % CORES
    where = jnp.stack([own_group, core, jnp.int32(groups)]).astype(jnp.int32)
    states = states_in.reshape(rows, SIZE, SIZE)

    line = lax.all_gather(
        step_inputs.reshape(count, SIZE), "tensor", axis=0, axis_index_groups=Z_LINES
    )
    outgoing = after(pack_states(states, migration_plan, own_group, groups), line)
    incoming = lax.all_to_all(outgoing, "group", 0, 0, tiled=True)
    incoming = incoming.reshape(groups * SLOTS, SIZE, SIZE)

    plane = lax.all_gather(line, "tensor", axis=0, axis_index_groups=X_RINGS)
    plane = plane.reshape(CHIPS, count, SIZE)
    other = lax.ppermute(plane, "tensor", CORE_SWAP)
    f32 = jnp.float32
    query, partial = pl.pallas_call(
        functools.partial(project_kernel, rows),
        out_shape=[jax.ShapeDtypeStruct((count, SIZE), f32)] * 2,
        in_specs=[SMEM, SMEM, SMEM, VMEM, VMEM, VMEM, VMEM],
        out_specs=[VMEM, VMEM],
        scratch_shapes=[pltpu.VMEM((count, SIZE), f32)],
        compiler_params=pltpu.CompilerParams(vmem_limit_bytes=24 * 2**20),
        cost_estimate=pl.CostEstimate(
            flops=2 * count * 4096 * 384, bytes_accessed=6 * 2**20, transcendentals=0
        ),
        name="project",
    )(where, migration_plan, head_decay, plane, other, jnp.transpose(qkv_weight, (1, 0, 2)), states)
    own, away = pl.pallas_call(
        functools.partial(finish_kernel, rows),
        out_shape=[
            jax.ShapeDtypeStruct((CHIPS, count, SIZE), f32),
            jax.ShapeDtypeStruct((CHIPS, count, SIZE), jnp.bfloat16),
        ],
        in_specs=[SMEM, SMEM, SMEM, SMEM, VMEM, VMEM, VMEM, VMEM, VMEM],
        out_specs=[VMEM, VMEM],
        scratch_shapes=[
            pltpu.VMEM((count, SIZE), f32),
            pltpu.VMEM((rows, SIZE), jnp.int32),
            pltpu.SMEM((MOVED,), jnp.int32),
            pltpu.SMEM((MOVED,), jnp.int32),
            pltpu.SMEM((groups,), jnp.int32),
        ],
        compiler_params=pltpu.CompilerParams(vmem_limit_bytes=24 * 2**20),
        cost_estimate=pl.CostEstimate(
            flops=2 * count * 4096 * 128, bytes_accessed=4 * 2**20, transcendentals=0
        ),
        name="finish",
    )(
        where, migration_plan, remaining_steps, head_decay, query, partial, incoming,
        head_gain.reshape(1, SIZE), out_weight,
    )
    received = lax.ppermute(away, "tensor", CORE_SWAP)
    plane = (own + received.astype(f32)).astype(jnp.bfloat16).reshape(XS, ZS, count, SIZE)
    pieces = lax.all_to_all(plane, "tensor", 0, 0, tiled=True, axis_index_groups=X_RINGS)
    line = jnp.sum(pieces.astype(f32), axis=0).astype(jnp.bfloat16)
    pieces = lax.all_to_all(line, "tensor", 0, 0, tiled=True, axis_index_groups=Z_LINES)
    result = jnp.sum(pieces.astype(f32), axis=0).astype(jnp.bfloat16)
    return result.reshape(STEPS, rows, SIZE)


def solution(mesh):
    placed = (
        P(None, "group", "tensor"),
        P(None, None, "tensor"),
        P("tensor", None),
        P("tensor"),
        P("tensor"),
        P("group", "tensor", None, None),
        P(),
        P(),
    )
    return jax.shard_map(
        body, mesh=mesh, in_specs=placed, out_specs=P(None, "group", "tensor"), check_vma=False
    )
```

```python
import functools

import jax
import jax.numpy as jnp
from jax import lax
from jax.experimental import pallas as pl
from jax.experimental.pallas import tpu as pltpu
from jax.sharding import PartitionSpec as P

STEPS = 4
SIZE = 128
MOVED = 13
XS, ZS, CORES = 4, 4, 2
CHIPS = XS * ZS
ZH, YS = 4, 4
SLOTS = 2
PASSING = 5


def tensor_id(x, z, c):
    return (x * ZS + z) * CORES + c


Z_LINES = [[tensor_id(x, z, c) for z in range(ZS)] for x in range(XS) for c in range(CORES)]
X_RINGS = [[tensor_id(x, z, c) for x in range(XS)] for z in range(ZS) for c in range(CORES)]
Y_RINGS = [[z * YS + y for y in range(YS)] for z in range(ZH)]
Z_RINGS = [[z * YS + y for z in range(ZH)] for y in range(YS)]
CORE_SWAP = [
    (tensor_id(x, z, c), tensor_id(x, z, 1 - c))
    for x in range(XS)
    for z in range(ZS)
    for c in range(CORES)
]

VMEM = pl.BlockSpec(memory_space=pltpu.VMEM)
SMEM = pl.BlockSpec(memory_space=pltpu.SMEM)
ANY = pl.BlockSpec(memory_space=pl.ANY)


def earlier(same):
    rows = same.shape[-1]
    before = jnp.arange(rows)[None, :] < jnp.arange(rows)[:, None]
    return jnp.sum((same & before).astype(jnp.int32), axis=-1)


def rows_out(migration_plan, own_group, groups, rows):
    plan = migration_plan.reshape(groups, rows)
    source = plan // rows
    here = source == own_group
    order = earlier(jnp.broadcast_to(here[:, None, :], (groups, rows, rows)))
    wanted = here[:, None, :] & (order[:, None, :] == jnp.arange(SLOTS)[None, :, None])
    chosen = jnp.sum(jnp.where(wanted, (plan % rows)[:, None, :], 0), axis=-1)
    return jnp.transpose(chosen.reshape(ZH, YS, SLOTS), (1, 0, 2)).reshape(-1)


def rows_on(migration_plan, own_group, groups, rows):
    plan = migration_plan.reshape(ZH, YS, rows)
    plan = lax.dynamic_index_in_dim(plan, own_group % YS, axis=1, keepdims=False)
    source = plan // rows
    target = jnp.arange(ZH) * YS + own_group % YS
    passing = (source // YS == own_group // YS) & (source != target[:, None])
    order = earlier(jnp.broadcast_to(passing[:, None, :], (ZH, rows, rows)))
    slot = earlier(source[:, :, None] == source[:, None, :])
    place = (source % YS) * (ZH * SLOTS) + jnp.arange(ZH)[:, None] * SLOTS + slot
    wanted = passing[:, None, :] & (order[:, None, :] == jnp.arange(PASSING)[None, :, None])
    return jnp.sum(jnp.where(wanted, place[:, None, :], 0), axis=-1).reshape(-1)


def pack_kernel(index_ref, states_ref, inputs_ref, out_ref, same_ref):
    for i in range(out_ref.shape[0]):
        out_ref[i] = states_ref[index_ref[i]].astype(jnp.bfloat16)
    same_ref[...] = inputs_ref[...]


def pass_kernel(index_ref, rows_ref, dep_ref, out_ref):
    for i in range(out_ref.shape[0]):
        out_ref[i] = rows_ref[index_ref[i]]


def split_rows(q):
    high = q.astype(jnp.bfloat16)
    low = (q - high.astype(jnp.float32)).astype(jnp.bfloat16)
    return jnp.concatenate([high, low], axis=0)


def project_kernel(
    rows, where_ref, plan_ref, decay_ref, own_ref, other_ref, weight_ref, states_ref,
    query_ref, partial_ref, kept_ref,
):
    group, core = where_ref[0], where_ref[1]
    count = STEPS * rows
    acc = [jnp.zeros((count, SIZE), jnp.float32) for _ in range(3)]
    for chip in range(CHIPS):
        a, b = own_ref[chip], other_ref[chip]
        even = jnp.where(core == 0, a, b)
        odd = jnp.where(core == 0, b, a)
        both = jnp.concatenate([even, odd], axis=1)
        for i in range(3):
            weight = weight_ref[i, 2 * SIZE * chip : 2 * SIZE * (chip + 1), :]
            acc[i] += jnp.dot(both, weight, preferred_element_type=jnp.float32)
    query = acc[0] / (1.0 + jnp.exp(-acc[0]))
    key = acc[1] / (1.0 + jnp.exp(-acc[1]))
    value = acc[2]
    query_ref[...] = query
    for row in range(rows):
        source = plan_ref[group * rows + row]
        state = states_ref[source % rows]
        high = state.astype(jnp.bfloat16)
        low = (state - high.astype(jnp.float32)).astype(jnp.bfloat16)
        mine = query_ref[pl.ds(row, STEPS, stride=rows), :]
        pair = split_rows(mine)
        first = jnp.dot(pair, high, preferred_element_type=jnp.float32)
        second = jnp.dot(pair[:STEPS], low, preferred_element_type=jnp.float32)
        product = first[:STEPS] + first[STEPS:] + second
        stays = (source // rows == group).astype(jnp.float32)
        kept_ref[pl.ds(row, STEPS, stride=rows), :] = product * stays
    decay = decay_ref[0]
    at = lambda x, t: x[t * rows : (t + 1) * rows]
    power = decay
    for t in range(STEPS):
        readout = power * at(kept_ref, t)
        power = power * decay
        weight = jnp.float32(1.0)
        for s in range(t, -1, -1):
            score = jnp.sum(at(query, t) * at(key, s), axis=-1, keepdims=True)
            readout = readout + (weight * score) * at(value, s)
            weight = weight * decay
        partial_ref[t * rows : (t + 1) * rows] = readout


def finish_kernel(
    rows, where_ref, plan_ref, remaining_ref, decay_ref, query_ref, partial_ref, incoming_ref,
    gain_ref, weight_ref, own_ref, other_ref, readout_ref, active_ref, row_ref, slot_ref, seen_ref,
):
    group, core = where_ref[0], where_ref[1]
    decay = decay_ref[0]
    for i in range(ZH):
        seen_ref[i] = 0
    for i in range(MOVED):
        row_ref[i] = 0
        slot_ref[i] = 0

    def scan(row, count):
        source = plan_ref[group * rows + row]
        source_group = source // rows
        moved = source_group != group
        place = jnp.minimum(count, MOVED - 1)

        @pl.when(moved)
        def _():
            far = source_group // YS
            rank = seen_ref[far]
            seen_ref[far] = rank + 1
            row_ref[place] = row
            slot_ref[place] = far * PASSING + jnp.minimum(rank, PASSING - 1)

        steps = remaining_ref[source]
        active_ref[pl.ds(row, 1), :] = jnp.full((1, SIZE), steps, jnp.int32)
        return count + moved.astype(jnp.int32)

    lax.fori_loop(0, rows, scan, 0)
    readout_ref[...] = partial_ref[...]
    power = lax.broadcasted_iota(jnp.int32, (STEPS, SIZE), 0)
    scale = jnp.where(power == 0, decay, 0.0)
    running = decay
    for t in range(1, STEPS):
        running = running * decay
        scale = jnp.where(power == t, running, scale)
    for i in range(MOVED):
        row = row_ref[i]
        mine = query_ref[pl.ds(row, STEPS, stride=rows), :]
        product = jnp.dot(
            split_rows(mine), incoming_ref[slot_ref[i]], preferred_element_type=jnp.float32
        )
        product = product[:STEPS] + product[STEPS:]
        readout_ref[pl.ds(row, STEPS, stride=rows), :] += scale * product
    pieces = []
    for t in range(STEPS):
        readout = readout_ref[t * rows : (t + 1) * rows]
        norm = lax.rsqrt(jnp.mean(readout * readout, axis=-1, keepdims=True) + 1e-05)
        normed = readout * norm * gain_ref[...]
        pieces.append(jnp.where(active_ref[...] > t, normed, 0.0))
    normed = jnp.concatenate(pieces, axis=0).astype(jnp.bfloat16)
    for chip in range(CHIPS):
        weight = weight_ref[:, 2 * SIZE * chip : 2 * SIZE * (chip + 1)]
        both = jnp.dot(normed, weight, preferred_element_type=jnp.float32)
        even, odd = both[:, :SIZE], both[:, SIZE:]
        own_ref[chip] = jnp.where(core == 0, even, odd)
        other_ref[chip] = jnp.where(core == 0, odd, even).astype(jnp.bfloat16)


def body(
    step_inputs,
    qkv_weight,
    out_weight,
    head_gain,
    head_decay,
    states_in,
    remaining_steps,
    migration_plan,
):
    rows = states_in.shape[0]
    count = STEPS * rows
    groups = lax.axis_size("group")
    own_group = lax.axis_index("group")
    core = lax.axis_index("tensor") % CORES
    where = jnp.stack([own_group, core]).astype(jnp.int32)
    states = states_in.reshape(rows, SIZE, SIZE)
    bf16, f32 = jnp.bfloat16, jnp.float32

    outgoing, inputs = pl.pallas_call(
        pack_kernel,
        out_shape=[
            jax.ShapeDtypeStruct((groups * SLOTS, SIZE, SIZE), bf16),
            jax.ShapeDtypeStruct((count, SIZE), bf16),
        ],
        in_specs=[SMEM, VMEM, VMEM],
        out_specs=[VMEM, VMEM],
        compiler_params=pltpu.CompilerParams(vmem_limit_bytes=16 * 2**20),
        name="pack",
    )(
        rows_out(migration_plan, own_group, groups, rows),
        states,
        step_inputs.reshape(count, SIZE),
    )
    passing = lax.all_to_all(outgoing, "group", 0, 0, tiled=True, axis_index_groups=Y_RINGS)
    line = lax.all_gather(inputs, "tensor", axis=0, axis_index_groups=Z_LINES)
    passing = pl.pallas_call(
        pass_kernel,
        out_shape=jax.ShapeDtypeStruct((ZH * PASSING, SIZE, SIZE), bf16),
        in_specs=[SMEM, VMEM, ANY],
        out_specs=VMEM,
        compiler_params=pltpu.CompilerParams(vmem_limit_bytes=16 * 2**20),
        name="pass_on",
    )(rows_on(migration_plan, own_group, groups, rows), passing, line)
    incoming = lax.all_to_all(passing, "group", 0, 0, tiled=True, axis_index_groups=Z_RINGS)

    plane = lax.all_gather(line, "tensor", axis=0, axis_index_groups=X_RINGS)
    plane = plane.reshape(CHIPS, count, SIZE)
    other = lax.ppermute(plane, "tensor", CORE_SWAP)
    query, partial = pl.pallas_call(
        functools.partial(project_kernel, rows),
        out_shape=[jax.ShapeDtypeStruct((count, SIZE), f32)] * 2,
        in_specs=[SMEM, SMEM, SMEM, VMEM, VMEM, VMEM, VMEM],
        out_specs=[VMEM, VMEM],
        scratch_shapes=[pltpu.VMEM((count, SIZE), f32)],
        compiler_params=pltpu.CompilerParams(vmem_limit_bytes=24 * 2**20),
        cost_estimate=pl.CostEstimate(
            flops=2 * count * 4096 * 384, bytes_accessed=6 * 2**20, transcendentals=0
        ),
        name="project",
    )(where, migration_plan, head_decay, plane, other, jnp.transpose(qkv_weight, (1, 0, 2)), states)
    own, away = pl.pallas_call(
        functools.partial(finish_kernel, rows),
        out_shape=[
            jax.ShapeDtypeStruct((CHIPS, count, SIZE), f32),
            jax.ShapeDtypeStruct((CHIPS, count, SIZE), jnp.bfloat16),
        ],
        in_specs=[SMEM, SMEM, SMEM, SMEM, VMEM, VMEM, VMEM, VMEM, VMEM],
        out_specs=[VMEM, VMEM],
        scratch_shapes=[
            pltpu.VMEM((count, SIZE), f32),
            pltpu.VMEM((rows, SIZE), jnp.int32),
            pltpu.SMEM((MOVED,), jnp.int32),
            pltpu.SMEM((MOVED,), jnp.int32),
            pltpu.SMEM((ZH,), jnp.int32),
        ],
        compiler_params=pltpu.CompilerParams(vmem_limit_bytes=24 * 2**20),
        cost_estimate=pl.CostEstimate(
            flops=2 * count * 4096 * 128, bytes_accessed=4 * 2**20, transcendentals=0
        ),
        name="finish",
    )(
        where, migration_plan, remaining_steps, head_decay, query, partial, incoming,
        head_gain.reshape(1, SIZE), out_weight,
    )
    received = lax.ppermute(away, "tensor", CORE_SWAP)
    plane = (own + received.astype(f32)).astype(jnp.bfloat16).reshape(XS, ZS, count, SIZE)
    pieces = lax.all_to_all(plane, "tensor", 0, 0, tiled=True, axis_index_groups=X_RINGS)
    line = jnp.sum(pieces.astype(f32), axis=0).astype(jnp.bfloat16)
    pieces = lax.all_to_all(line, "tensor", 0, 0, tiled=True, axis_index_groups=Z_LINES)
    result = jnp.sum(pieces.astype(f32), axis=0).astype(jnp.bfloat16)
    return result.reshape(STEPS, rows, SIZE)


def solution(mesh):
    placed = (
        P(None, "group", "tensor"),
        P(None, None, "tensor"),
        P("tensor", None),
        P("tensor"),
        P("tensor"),
        P("group", "tensor", None, None),
        P(),
        P(),
    )
    return jax.shard_map(
        body, mesh=mesh, in_specs=placed, out_specs=P(None, "group", "tensor"), check_vma=False
    )
```

```python
import functools

import jax
import jax.numpy as jnp
from jax import lax
from jax.experimental import pallas as pl
from jax.experimental.pallas import tpu as pltpu
from jax.sharding import PartitionSpec as P

STEPS = 4
SIZE = 128
MOVED = 13
XS, ZS, CORES = 4, 4, 2
CHIPS = XS * ZS
ZH, YS = 4, 4
SLOTS = 2
CODE = 64
PASSING = 5


def tensor_id(x, z, c):
    return (x * ZS + z) * CORES + c


SPOTS = [(x, z, c) for x in range(XS) for z in range(ZS) for c in range(CORES)]
Z_LINES = [[tensor_id(x, z, c) for z in range(ZS)] for x in range(XS) for c in range(CORES)]
X_RINGS = [[tensor_id(x, z, c) for x in range(XS)] for z in range(ZS) for c in range(CORES)]
CORE_SWAP = [(tensor_id(x, z, c), tensor_id(x, z, 1 - c)) for x, z, c in SPOTS]
X_SHIFTS = [
    [(tensor_id(x, z, c), tensor_id((x + k) % XS, z, c)) for x, z, c in SPOTS] for k in range(XS)
]
Y_RINGS = [[z * YS + y for y in range(YS)] for z in range(ZH)]
Z_RINGS = [[z * YS + y for z in range(ZH)] for y in range(YS)]

VMEM = pl.BlockSpec(memory_space=pltpu.VMEM)
SMEM = pl.BlockSpec(memory_space=pltpu.SMEM)
ANY = pl.BlockSpec(memory_space=pl.ANY)
SMALL = pltpu.CompilerParams(vmem_limit_bytes=16 * 2**20)
ROOMY = pltpu.CompilerParams(vmem_limit_bytes=56 * 2**20)
DMA = pltpu.SemaphoreType.DMA


def after_kernel(x_ref, dep_ref, out_ref):
    pass


def after(x, dep):
    return pl.pallas_call(
        after_kernel,
        out_shape=jax.ShapeDtypeStruct(x.shape, x.dtype),
        in_specs=[ANY, ANY],
        out_specs=ANY,
        input_output_aliases={0: 0},
        name="after",
    )(x, dep)


def targets(migration_plan, own_group, rows):
    wanted = migration_plan[None, :] == (own_group * rows + jnp.arange(rows))[:, None]
    return jnp.sum(jnp.where(wanted, jnp.arange(migration_plan.shape[0])[None, :], 0), axis=1)


def rows_on(migration_plan, own_group, groups, rows):
    plan = migration_plan.reshape(ZH, YS, rows)
    plan = lax.dynamic_index_in_dim(plan, own_group % YS, axis=1, keepdims=False)
    source = plan // rows
    target = jnp.arange(ZH) * YS + own_group % YS
    passing = (source // YS == own_group // YS) & (source != target[:, None])
    before = jnp.arange(rows)[None, :] < jnp.arange(rows)[:, None]
    order = jnp.sum((passing[:, None, :] & before).astype(jnp.int32), axis=-1)
    same = source[:, :, None] == source[:, None, :]
    slot = jnp.sum((same & (plan[:, None, :] < plan[:, :, None])).astype(jnp.int32), axis=-1)
    place = (source % YS) * (ZH * SLOTS) + jnp.arange(ZH)[:, None] * SLOTS + slot
    wanted = passing[:, None, :] & (order[:, None, :] == jnp.arange(PASSING)[None, :, None])
    place = jnp.sum(jnp.where(wanted, place[:, None, :], 0), axis=-1)
    return jnp.clip(place, 0, groups * SLOTS - 1).reshape(-1)


def pack_kernel(
    rows, target_ref, states_ref, inputs_ref, out_ref, same_ref,
    wide_ref, narrow_ref, inputs_vmem, slot_ref, seen_ref, in_sem, out_sem, copy_sem,
):
    group = group_here()
    load = pltpu.make_async_copy(inputs_ref, inputs_vmem, copy_sem.at[0])
    load.start()
    for i in range(ZH * YS):
        seen_ref[i] = 0

    def scan(row, count):
        goal = target_ref[row] // rows
        leaves = (goal != group) & (count < MOVED)

        @pl.when(leaves)
        def _():
            rank = seen_ref[goal]
            seen_ref[goal] = rank + 1
            slot_ref[count] = (
                (goal % YS) * (ZH * SLOTS) + goal // YS * SLOTS + jnp.minimum(rank, SLOTS - 1)
            )
            pltpu.make_async_copy(
                states_ref.at[row], wide_ref.at[count], in_sem.at[count]
            ).start()

        return count + leaves.astype(jnp.int32)

    count = lax.fori_loop(0, rows, scan, jnp.int32(0), unroll=8)
    load.wait()
    store = pltpu.make_async_copy(inputs_vmem, same_ref, copy_sem.at[1])
    store.start()
    for i in range(MOVED):

        @pl.when(i < count)
        def _(i=i):
            pltpu.make_async_copy(states_ref.at[0], wide_ref.at[i], in_sem.at[i]).wait()
            narrow_ref[i] = wide_ref[i].astype(jnp.bfloat16)
            pltpu.make_async_copy(
                narrow_ref.at[i], out_ref.at[slot_ref[i]], out_sem.at[i]
            ).start()

    for i in range(MOVED):

        @pl.when(i < count)
        def _(i=i):
            pltpu.make_async_copy(narrow_ref.at[i], out_ref.at[0], out_sem.at[i]).wait()

    store.wait()


def pass_kernel(index_ref, rows_ref, dep_ref, out_ref, sem):
    copies = [
        pltpu.make_async_copy(rows_ref.at[index_ref[i]], out_ref.at[i], sem.at[i])
        for i in range(out_ref.shape[0])
    ]
    for copy in copies:
        copy.start()
    for copy in copies:
        copy.wait()


def group_here():
    return lax.axis_index("group")


def core_here():
    return lax.rem(lax.axis_index("tensor"), CORES)


def x_here():
    return lax.div(lax.axis_index("tensor"), CORES * ZS)


def deal_kernel(weight_ref, dep_ref, *out_refs):
    x = x_here()
    width = weight_ref.shape[1] // XS
    for k in range(XS):
        start = pl.multiple_of(lax.rem(x + k, XS) * width, width)
        out_refs[k][...] = weight_ref[:, pl.ds(start, width)]


def split_rows(q):
    high = q.astype(jnp.bfloat16)
    low = (q - high.astype(jnp.float32)).astype(jnp.bfloat16)
    return jnp.concatenate([high, low], axis=0)


def project_kernel(
    rows, plan_ref, remaining_ref, decay_ref, gain_ref, own_ref, other_ref, weight_ref,
    states_ref, scaled_ref, partial_ref, gains_ref, code_ref, query_ref, kept_ref, active_ref,
    seen_ref,
):
    group, core = group_here(), core_here()
    count = STEPS * rows
    for i in range(ZH):
        seen_ref[i] = 0
    for i in range(code_ref.shape[0]):
        code_ref[i] = rows * CODE
    found = jnp.int32(0)
    for row in range(rows):
        source = plan_ref[group * rows + row]
        source_group = source // rows
        moved = (source_group != group) & (found < MOVED)
        far = source_group // YS
        rank = seen_ref[far]
        slot = far * PASSING + jnp.minimum(rank, PASSING - 1)
        step = moved.astype(jnp.int32)
        seen_ref[far] = rank + step
        code_ref[found] = jnp.where(moved, row * CODE + slot, rows * CODE)
        found = found + step
        active_ref[row : row + 1, :] = jnp.full((1, SIZE), remaining_ref[source], jnp.int32)
    acc = [jnp.zeros((count, SIZE), jnp.float32) for _ in range(3)]
    for chip in range(CHIPS):
        a, b = own_ref[chip], other_ref[chip]
        even = jnp.where(core == 0, a, b)
        odd = jnp.where(core == 0, b, a)
        both = jnp.concatenate([even, odd], axis=1)
        for i in range(3):
            weight = weight_ref[i, 2 * SIZE * chip : 2 * SIZE * (chip + 1), :]
            acc[i] += jnp.dot(both, weight, preferred_element_type=jnp.float32)
    query = acc[0] / (1.0 + jnp.exp(-acc[0]))
    key = acc[1] / (1.0 + jnp.exp(-acc[1]))
    value = acc[2]
    query_ref[...] = query
    for row in range(rows):
        source = plan_ref[group * rows + row]
        state = states_ref[source % rows]
        high = state.astype(jnp.bfloat16)
        low = (state - high.astype(jnp.float32)).astype(jnp.bfloat16)
        mine = query_ref[pl.ds(row, STEPS, stride=rows), :]
        pair = split_rows(mine)
        first = jnp.dot(pair, high, preferred_element_type=jnp.float32)
        second = jnp.dot(pair[:STEPS], low, preferred_element_type=jnp.float32)
        product = first[:STEPS] + first[STEPS:] + second
        stays = (source // rows == group).astype(jnp.float32)
        kept_ref[pl.ds(row, STEPS, stride=rows), :] = product * stays
    decay = decay_ref[0]
    at = lambda x, t: x[t * rows : (t + 1) * rows]
    power = decay
    for t in range(STEPS):
        here = slice(t * rows, (t + 1) * rows)
        scaled_ref[here] = power * at(query, t)
        readout = power * kept_ref[here]
        power = power * decay
        weight = jnp.float32(1.0)
        for s in range(t, -1, -1):
            score = jnp.sum(at(query, t) * at(key, s), axis=-1, keepdims=True)
            readout = readout + (weight * score) * at(value, s)
            weight = weight * decay
        partial_ref[here] = readout
        gains_ref[here] = jnp.where(active_ref[...] > t, gain_ref[...], 0.0)


def finish_kernel(
    rows, code_ref, scaled_ref, partial_ref, gains_ref, incoming_ref, normed_ref, moved_ref
):
    room = moved_ref.shape[0] // STEPS
    moved_ref[...] = jnp.zeros_like(moved_ref)
    for i in range(MOVED):
        row = lax.div(code_ref[i], CODE)
        mine = scaled_ref[pl.ds(jnp.minimum(row, rows - 1), STEPS, stride=rows), :]
        state = incoming_ref[lax.rem(code_ref[i], CODE)]
        product = jnp.dot(split_rows(mine), state, preferred_element_type=jnp.float32)
        moved_ref[pl.ds(row, STEPS, stride=room), :] = product[:STEPS] + product[STEPS:]
    for t in range(STEPS):
        here = slice(t * rows, (t + 1) * rows)
        readout = partial_ref[here] + moved_ref[t * room : t * room + rows]
        norm = lax.rsqrt(jnp.mean(readout * readout, axis=-1, keepdims=True) + 1e-05)
        normed_ref[here] = (readout * norm * gains_ref[here]).astype(jnp.bfloat16)


def output_kernel(ring_ref, *refs):
    weights, (own_ref, other_ref) = refs[:XS], refs[XS:]
    core, x = core_here(), x_here()
    rows = [ring_ref[lax.rem(x + XS - k, XS)] for k in range(XS)]
    pairs = [
        (jnp.concatenate(rows[k : k + 2], axis=1), weights[k], weights[k + 1])
        for k in range(0, XS, 2)
    ]
    width = CORES * SIZE
    for z in range(ZS):
        part = slice(z * width, (z + 1) * width)
        total = 0.0
        for both, first, second in pairs:
            weight = jnp.concatenate([first[:, part], second[:, part]], axis=0)
            total = total + jnp.dot(both, weight, preferred_element_type=jnp.float32)
        even, odd = total[:, :SIZE], total[:, SIZE:]
        own_ref[z] = jnp.where(core == 0, even, odd)
        other_ref[z] = jnp.where(core == 0, odd, even).astype(jnp.bfloat16)


def body(
    step_inputs,
    qkv_weight,
    out_weight,
    head_gain,
    head_decay,
    states_in,
    remaining_steps,
    migration_plan,
):
    rows = states_in.shape[0]
    count = STEPS * rows
    groups = lax.axis_size("group")
    own_group = lax.axis_index("group")
    states = states_in.reshape(rows, SIZE, SIZE)
    bf16, f32 = jnp.bfloat16, jnp.float32

    outgoing, inputs = pl.pallas_call(
        functools.partial(pack_kernel, rows),
        out_shape=[
            jax.ShapeDtypeStruct((groups * SLOTS, SIZE, SIZE), bf16),
            jax.ShapeDtypeStruct((count, SIZE), bf16),
        ],
        in_specs=[SMEM, ANY, ANY],
        out_specs=[ANY, ANY],
        scratch_shapes=[
            pltpu.VMEM((MOVED, SIZE, SIZE), f32),
            pltpu.VMEM((MOVED, SIZE, SIZE), bf16),
            pltpu.VMEM((count, SIZE), bf16),
            pltpu.SMEM((MOVED,), jnp.int32),
            pltpu.SMEM((ZH * YS,), jnp.int32),
            DMA((MOVED,)),
            DMA((MOVED,)),
            DMA((2,)),
        ],
        compiler_params=ROOMY,
        name="pack",
    )(targets(migration_plan, own_group, rows), states, step_inputs.reshape(count, SIZE))
    passing = lax.all_to_all(outgoing, "group", 0, 0, tiled=True, axis_index_groups=Y_RINGS)
    line = lax.all_gather(inputs, "tensor", axis=0, axis_index_groups=Z_LINES)
    passing = pl.pallas_call(
        pass_kernel,
        out_shape=jax.ShapeDtypeStruct((ZH * PASSING, SIZE, SIZE), bf16),
        in_specs=[SMEM, VMEM, ANY],
        out_specs=ANY,
        scratch_shapes=[DMA((ZH * PASSING,))],
        compiler_params=SMALL,
        name="pass_on",
    )(rows_on(migration_plan, own_group, groups, rows), passing, line)
    incoming = lax.all_to_all(passing, "group", 0, 0, tiled=True, axis_index_groups=Z_RINGS)

    plane = lax.all_gather(after(line, passing), "tensor", axis=0, axis_index_groups=X_RINGS)
    plane = plane.reshape(CHIPS, count, SIZE)
    other = lax.ppermute(plane, "tensor", CORE_SWAP)
    scaled, partial, gains, code = pl.pallas_call(
        functools.partial(project_kernel, rows),
        out_shape=[
            jax.ShapeDtypeStruct((count, SIZE), f32),
            jax.ShapeDtypeStruct((count, SIZE), f32),
            jax.ShapeDtypeStruct((count, SIZE), f32),
            jax.ShapeDtypeStruct((MOVED + 1,), jnp.int32),
        ],
        in_specs=[SMEM, SMEM, SMEM, VMEM, VMEM, VMEM, VMEM, VMEM],
        out_specs=[VMEM, VMEM, VMEM, SMEM],
        scratch_shapes=[
            pltpu.VMEM((count, SIZE), f32),
            pltpu.VMEM((count, SIZE), f32),
            pltpu.VMEM((rows, SIZE), jnp.int32),
            pltpu.SMEM((ZH,), jnp.int32),
        ],
        compiler_params=pltpu.CompilerParams(vmem_limit_bytes=24 * 2**20),
        cost_estimate=pl.CostEstimate(
            flops=2 * count * 4096 * 384, bytes_accessed=6 * 2**20, transcendentals=0
        ),
        name="project",
    )(
        migration_plan, remaining_steps, head_decay, head_gain.reshape(1, SIZE), plane, other,
        jnp.transpose(qkv_weight, (1, 0, 2)), states,
    )

    dealt = pl.pallas_call(
        deal_kernel,
        out_shape=[jax.ShapeDtypeStruct((SIZE, out_weight.shape[1] // XS), bf16)] * XS,
        in_specs=[VMEM, ANY],
        out_specs=[VMEM] * XS,
        compiler_params=SMALL,
        name="deal",
    )(out_weight, plane)
    dealt = [dealt[0]] + [lax.ppermute(dealt[k], "tensor", X_SHIFTS[k]) for k in range(1, XS)]

    normed = pl.pallas_call(
        functools.partial(finish_kernel, rows),
        out_shape=jax.ShapeDtypeStruct((count, SIZE), bf16),
        in_specs=[SMEM, VMEM, VMEM, VMEM, VMEM],
        out_specs=VMEM,
        scratch_shapes=[pltpu.VMEM((STEPS * (rows + 8), SIZE), f32)],
        compiler_params=SMALL,
        name="finish",
    )(code, scaled, partial, gains, incoming)
    ring = lax.all_gather(normed, "tensor", axis=0, axis_index_groups=X_RINGS)
    own, away = pl.pallas_call(
        output_kernel,
        out_shape=[
            jax.ShapeDtypeStruct((ZS, count, SIZE), f32),
            jax.ShapeDtypeStruct((ZS, count, SIZE), bf16),
        ],
        in_specs=[VMEM] * (1 + XS),
        out_specs=[VMEM, VMEM],
        compiler_params=SMALL,
        name="output",
    )(ring, *dealt)
    received = lax.ppermute(away, "tensor", CORE_SWAP)
    sums = (own + received.astype(f32)).astype(bf16)
    pieces = lax.all_to_all(sums, "tensor", 0, 0, tiled=True, axis_index_groups=Z_LINES)
    result = jnp.sum(pieces.astype(f32), axis=0).astype(bf16)
    return result.reshape(STEPS, rows, SIZE)


def solution(mesh):
    placed = (
        P(None, "group", "tensor"),
        P(None, None, "tensor"),
        P("tensor", None),
        P("tensor"),
        P("tensor"),
        P("group", "tensor", None, None),
        P(),
        P(),
    )
    return jax.shard_map(
        body, mesh=mesh, in_specs=placed, out_specs=P(None, "group", "tensor"), check_vma=False
    )
```

```python
import functools

import jax
import jax.numpy as jnp
from jax import lax
from jax.experimental import pallas as pl
from jax.experimental.pallas import tpu as pltpu
from jax.sharding import PartitionSpec as P

STEPS = 4
SIZE = 128
MOVED = 13
XS, ZS, CORES = 4, 4, 2
CHIPS = XS * ZS
ZH, YS = 4, 4
SLOTS = 2
CODE = 64
PASSING = 5


def tensor_id(x, z, c):
    return (x * ZS + z) * CORES + c


SPOTS = [(x, z, c) for x in range(XS) for z in range(ZS) for c in range(CORES)]
Z_LINES = [[tensor_id(x, z, c) for z in range(ZS)] for x in range(XS) for c in range(CORES)]
X_RINGS = [[tensor_id(x, z, c) for x in range(XS)] for z in range(ZS) for c in range(CORES)]
X_CORES = [[tensor_id(x, z, c) for x in range(XS) for c in range(CORES)] for z in range(ZS)]
CORE_SWAP = [(tensor_id(x, z, c), tensor_id(x, z, 1 - c)) for x, z, c in SPOTS]
X_SHIFTS = [
    [(tensor_id(x, z, c), tensor_id((x + k) % XS, z, c)) for x, z, c in SPOTS] for k in range(XS)
]
Y_RINGS = [[z * YS + y for y in range(YS)] for z in range(ZH)]
Z_RINGS = [[z * YS + y for z in range(ZH)] for y in range(YS)]

VMEM = pl.BlockSpec(memory_space=pltpu.VMEM)
SMEM = pl.BlockSpec(memory_space=pltpu.SMEM)
ANY = pl.BlockSpec(memory_space=pl.ANY)
SMALL = pltpu.CompilerParams(vmem_limit_bytes=16 * 2**20)
ROOMY = pltpu.CompilerParams(vmem_limit_bytes=56 * 2**20)
DMA = pltpu.SemaphoreType.DMA


def after_kernel(x_ref, dep_ref, out_ref):
    pass


def after(x, dep):
    return pl.pallas_call(
        after_kernel,
        out_shape=jax.ShapeDtypeStruct(x.shape, x.dtype),
        in_specs=[ANY, ANY],
        out_specs=ANY,
        input_output_aliases={0: 0},
        name="after",
    )(x, dep)


def targets(migration_plan, own_group, rows):
    wanted = migration_plan[None, :] == (own_group * rows + jnp.arange(rows))[:, None]
    return jnp.sum(jnp.where(wanted, jnp.arange(migration_plan.shape[0])[None, :], 0), axis=1)


def rows_on(migration_plan, own_group, groups, rows):
    plan = migration_plan.reshape(ZH, YS, rows)
    plan = lax.dynamic_index_in_dim(plan, own_group % YS, axis=1, keepdims=False)
    source = plan // rows
    target = jnp.arange(ZH) * YS + own_group % YS
    passing = (source // YS == own_group // YS) & (source != target[:, None])
    before = jnp.arange(rows)[None, :] < jnp.arange(rows)[:, None]
    order = jnp.sum((passing[:, None, :] & before).astype(jnp.int32), axis=-1)
    same = source[:, :, None] == source[:, None, :]
    slot = jnp.sum((same & (plan[:, None, :] < plan[:, :, None])).astype(jnp.int32), axis=-1)
    place = (source % YS) * (ZH * SLOTS) + jnp.arange(ZH)[:, None] * SLOTS + slot
    wanted = passing[:, None, :] & (order[:, None, :] == jnp.arange(PASSING)[None, :, None])
    place = jnp.sum(jnp.where(wanted, place[:, None, :], 0), axis=-1)
    return jnp.clip(place, 0, groups * SLOTS - 1).reshape(-1)


def pack_kernel(
    rows, target_ref, states_ref, inputs_ref, out_ref, same_ref,
    wide_ref, narrow_ref, inputs_vmem, slot_ref, seen_ref, in_sem, out_sem, copy_sem,
):
    group = group_here()
    load = pltpu.make_async_copy(inputs_ref, inputs_vmem, copy_sem.at[0])
    load.start()
    for i in range(ZH * YS):
        seen_ref[i] = 0

    def scan(row, count):
        goal = target_ref[row] // rows
        leaves = (goal != group) & (count < MOVED)

        @pl.when(leaves)
        def _():
            rank = seen_ref[goal]
            seen_ref[goal] = rank + 1
            slot_ref[count] = (
                (goal % YS) * (ZH * SLOTS) + goal // YS * SLOTS + jnp.minimum(rank, SLOTS - 1)
            )
            pltpu.make_async_copy(
                states_ref.at[row], wide_ref.at[count], in_sem.at[count]
            ).start()

        return count + leaves.astype(jnp.int32)

    count = lax.fori_loop(0, rows, scan, jnp.int32(0), unroll=8)
    load.wait()
    store = pltpu.make_async_copy(inputs_vmem, same_ref, copy_sem.at[1])
    store.start()
    for i in range(MOVED):

        @pl.when(i < count)
        def _(i=i):
            pltpu.make_async_copy(states_ref.at[0], wide_ref.at[i], in_sem.at[i]).wait()
            narrow_ref[i] = wide_ref[i].astype(jnp.bfloat16)
            pltpu.make_async_copy(
                narrow_ref.at[i], out_ref.at[slot_ref[i]], out_sem.at[i]
            ).start()

    for i in range(MOVED):

        @pl.when(i < count)
        def _(i=i):
            pltpu.make_async_copy(narrow_ref.at[i], out_ref.at[0], out_sem.at[i]).wait()

    store.wait()


def pass_kernel(index_ref, rows_ref, dep_ref, out_ref, sem):
    copies = [
        pltpu.make_async_copy(rows_ref.at[index_ref[i]], out_ref.at[i], sem.at[i])
        for i in range(out_ref.shape[0])
    ]
    for copy in copies:
        copy.start()
    for copy in copies:
        copy.wait()


def group_here():
    return lax.axis_index("group")


def core_here():
    return lax.rem(lax.axis_index("tensor"), CORES)


def x_here():
    return lax.div(lax.axis_index("tensor"), CORES * ZS)


def columns(shift, z, core):
    spot = (lax.rem(x_here() + shift, XS) * ZS + z) * CORES + core
    return pl.ds(pl.multiple_of(spot * SIZE, SIZE), SIZE)


def lend_kernel(weight_ref, dep_ref, out_ref):
    other = 1 - core_here()
    for k in range(XS):
        for z in range(ZS):
            out_ref[k, z] = weight_ref[:, columns(k, z, other)]


def deal_kernel(weight_ref, lent_ref, *out_refs):
    core = core_here()
    for k in range(XS):
        for z in range(ZS):
            own, lent = weight_ref[:, columns(k, z, core)], lent_ref[k, z]
            out_refs[k][z, :SIZE] = jnp.where(core == 0, own, lent)
            out_refs[k][z, SIZE:] = jnp.where(core == 0, lent, own)


def split_rows(q):
    high = q.astype(jnp.bfloat16)
    low = (q - high.astype(jnp.float32)).astype(jnp.bfloat16)
    return jnp.concatenate([high, low], axis=0)


def project_kernel(
    rows, plan_ref, remaining_ref, decay_ref, gain_ref, own_ref, other_ref, weight_ref,
    states_ref, scaled_ref, partial_ref, gains_ref, code_ref, query_ref, kept_ref, active_ref,
    seen_ref,
):
    group, core = group_here(), core_here()
    count = STEPS * rows
    for i in range(ZH):
        seen_ref[i] = 0
    for i in range(code_ref.shape[0]):
        code_ref[i] = rows * CODE
    found = jnp.int32(0)
    for row in range(rows):
        source = plan_ref[group * rows + row]
        source_group = source // rows
        moved = (source_group != group) & (found < MOVED)
        far = source_group // YS
        rank = seen_ref[far]
        slot = far * PASSING + jnp.minimum(rank, PASSING - 1)
        step = moved.astype(jnp.int32)
        seen_ref[far] = rank + step
        code_ref[found] = jnp.where(moved, row * CODE + slot, rows * CODE)
        found = found + step
        active_ref[row : row + 1, :] = jnp.full((1, SIZE), remaining_ref[source], jnp.int32)
    acc = [jnp.zeros((count, SIZE), jnp.float32) for _ in range(3)]
    for chip in range(CHIPS):
        a, b = own_ref[chip], other_ref[chip]
        even = jnp.where(core == 0, a, b)
        odd = jnp.where(core == 0, b, a)
        both = jnp.concatenate([even, odd], axis=1)
        for i in range(3):
            weight = weight_ref[i, 2 * SIZE * chip : 2 * SIZE * (chip + 1), :]
            acc[i] += jnp.dot(both, weight, preferred_element_type=jnp.float32)
    query = acc[0] / (1.0 + jnp.exp(-acc[0]))
    key = acc[1] / (1.0 + jnp.exp(-acc[1]))
    value = acc[2]
    query_ref[...] = query
    for row in range(rows):
        source = plan_ref[group * rows + row]
        state = states_ref[source % rows]
        high = state.astype(jnp.bfloat16)
        low = (state - high.astype(jnp.float32)).astype(jnp.bfloat16)
        mine = query_ref[pl.ds(row, STEPS, stride=rows), :]
        pair = split_rows(mine)
        first = jnp.dot(pair, high, preferred_element_type=jnp.float32)
        second = jnp.dot(pair[:STEPS], low, preferred_element_type=jnp.float32)
        product = first[:STEPS] + first[STEPS:] + second
        stays = (source // rows == group).astype(jnp.float32)
        kept_ref[pl.ds(row, STEPS, stride=rows), :] = product * stays
    decay = decay_ref[0]
    at = lambda x, t: x[t * rows : (t + 1) * rows]
    power = decay
    for t in range(STEPS):
        here = slice(t * rows, (t + 1) * rows)
        scaled_ref[here] = power * at(query, t)
        readout = power * kept_ref[here]
        power = power * decay
        weight = jnp.float32(1.0)
        for s in range(t, -1, -1):
            score = jnp.sum(at(query, t) * at(key, s), axis=-1, keepdims=True)
            readout = readout + (weight * score) * at(value, s)
            weight = weight * decay
        partial_ref[here] = readout
        gains_ref[here] = jnp.where(active_ref[...] > t, gain_ref[...], 0.0)


def finish_kernel(
    rows, code_ref, scaled_ref, partial_ref, gains_ref, incoming_ref, normed_ref, moved_ref
):
    room = moved_ref.shape[0] // STEPS
    moved_ref[...] = jnp.zeros_like(moved_ref)
    for i in range(MOVED):
        row = lax.div(code_ref[i], CODE)
        mine = scaled_ref[pl.ds(jnp.minimum(row, rows - 1), STEPS, stride=rows), :]
        state = incoming_ref[lax.rem(code_ref[i], CODE)]
        product = jnp.dot(split_rows(mine), state, preferred_element_type=jnp.float32)
        moved_ref[pl.ds(row, STEPS, stride=room), :] = product[:STEPS] + product[STEPS:]
    for t in range(STEPS):
        here = slice(t * rows, (t + 1) * rows)
        readout = partial_ref[here] + moved_ref[t * room : t * room + rows]
        norm = lax.rsqrt(jnp.mean(readout * readout, axis=-1, keepdims=True) + 1e-05)
        normed_ref[here] = (readout * norm * gains_ref[here]).astype(jnp.bfloat16)


def output_kernel(ring_ref, *refs):
    weights, out_ref = refs[:XS], refs[XS]
    x = x_here()
    sources = [lax.rem(x + XS - k, XS) * CORES for k in range(XS)]
    rows = [
        jnp.concatenate([ring_ref[source + c] for c in range(CORES)], axis=1) for source in sources
    ]
    for z in range(ZS):
        total = 0.0
        for k in range(XS):
            total = total + jnp.dot(rows[k], weights[k][z], preferred_element_type=jnp.float32)
        out_ref[z] = total.astype(jnp.bfloat16)


def body(
    step_inputs,
    qkv_weight,
    out_weight,
    head_gain,
    head_decay,
    states_in,
    remaining_steps,
    migration_plan,
):
    rows = states_in.shape[0]
    count = STEPS * rows
    groups = lax.axis_size("group")
    own_group = lax.axis_index("group")
    states = states_in.reshape(rows, SIZE, SIZE)
    bf16, f32 = jnp.bfloat16, jnp.float32

    outgoing, inputs = pl.pallas_call(
        functools.partial(pack_kernel, rows),
        out_shape=[
            jax.ShapeDtypeStruct((groups * SLOTS, SIZE, SIZE), bf16),
            jax.ShapeDtypeStruct((count, SIZE), bf16),
        ],
        in_specs=[SMEM, ANY, ANY],
        out_specs=[ANY, ANY],
        scratch_shapes=[
            pltpu.VMEM((MOVED, SIZE, SIZE), f32),
            pltpu.VMEM((MOVED, SIZE, SIZE), bf16),
            pltpu.VMEM((count, SIZE), bf16),
            pltpu.SMEM((MOVED,), jnp.int32),
            pltpu.SMEM((ZH * YS,), jnp.int32),
            DMA((MOVED,)),
            DMA((MOVED,)),
            DMA((2,)),
        ],
        compiler_params=ROOMY,
        name="pack",
    )(targets(migration_plan, own_group, rows), states, step_inputs.reshape(count, SIZE))
    passing = lax.all_to_all(outgoing, "group", 0, 0, tiled=True, axis_index_groups=Y_RINGS)
    line = lax.all_gather(inputs, "tensor", axis=0, axis_index_groups=Z_LINES)
    passing = pl.pallas_call(
        pass_kernel,
        out_shape=jax.ShapeDtypeStruct((ZH * PASSING, SIZE, SIZE), bf16),
        in_specs=[SMEM, VMEM, ANY],
        out_specs=ANY,
        scratch_shapes=[DMA((ZH * PASSING,))],
        compiler_params=SMALL,
        name="pass_on",
    )(rows_on(migration_plan, own_group, groups, rows), passing, line)
    incoming = lax.all_to_all(passing, "group", 0, 0, tiled=True, axis_index_groups=Z_RINGS)

    plane = lax.all_gather(after(line, passing), "tensor", axis=0, axis_index_groups=X_RINGS)
    plane = plane.reshape(CHIPS, count, SIZE)
    other = lax.ppermute(plane, "tensor", CORE_SWAP)
    scaled, partial, gains, code = pl.pallas_call(
        functools.partial(project_kernel, rows),
        out_shape=[
            jax.ShapeDtypeStruct((count, SIZE), f32),
            jax.ShapeDtypeStruct((count, SIZE), f32),
            jax.ShapeDtypeStruct((count, SIZE), f32),
            jax.ShapeDtypeStruct((MOVED + 1,), jnp.int32),
        ],
        in_specs=[SMEM, SMEM, SMEM, VMEM, VMEM, VMEM, VMEM, VMEM],
        out_specs=[VMEM, VMEM, VMEM, SMEM],
        scratch_shapes=[
            pltpu.VMEM((count, SIZE), f32),
            pltpu.VMEM((count, SIZE), f32),
            pltpu.VMEM((rows, SIZE), jnp.int32),
            pltpu.SMEM((ZH,), jnp.int32),
        ],
        compiler_params=pltpu.CompilerParams(vmem_limit_bytes=24 * 2**20),
        cost_estimate=pl.CostEstimate(
            flops=2 * count * 4096 * 384, bytes_accessed=6 * 2**20, transcendentals=0
        ),
        name="project",
    )(
        migration_plan, remaining_steps, head_decay, head_gain.reshape(1, SIZE), plane, other,
        jnp.transpose(qkv_weight, (1, 0, 2)), states,
    )

    lent = pl.pallas_call(
        lend_kernel,
        out_shape=jax.ShapeDtypeStruct((XS, ZS, SIZE, SIZE), bf16),
        in_specs=[VMEM, ANY],
        out_specs=VMEM,
        compiler_params=SMALL,
        name="lend",
    )(out_weight, passing)
    lent = lax.ppermute(lent, "tensor", CORE_SWAP)
    dealt = pl.pallas_call(
        deal_kernel,
        out_shape=[jax.ShapeDtypeStruct((ZS, CORES * SIZE, SIZE), bf16)] * XS,
        in_specs=[VMEM, VMEM],
        out_specs=[VMEM] * XS,
        compiler_params=SMALL,
        name="deal",
    )(out_weight, lent)
    dealt = [dealt[0]] + [lax.ppermute(dealt[k], "tensor", X_SHIFTS[k]) for k in range(1, XS)]

    normed = pl.pallas_call(
        functools.partial(finish_kernel, rows),
        out_shape=jax.ShapeDtypeStruct((count, SIZE), bf16),
        in_specs=[SMEM, VMEM, VMEM, VMEM, VMEM],
        out_specs=VMEM,
        scratch_shapes=[pltpu.VMEM((STEPS * (rows + 8), SIZE), f32)],
        compiler_params=SMALL,
        name="finish",
    )(code, scaled, partial, gains, incoming)
    ring = lax.all_gather(normed, "tensor", axis=0, axis_index_groups=X_CORES)
    sums = pl.pallas_call(
        output_kernel,
        out_shape=jax.ShapeDtypeStruct((ZS, count, SIZE), bf16),
        in_specs=[VMEM] * (1 + XS),
        out_specs=VMEM,
        compiler_params=SMALL,
        name="output",
    )(ring, *dealt)
    pieces = lax.all_to_all(sums, "tensor", 0, 0, tiled=True, axis_index_groups=Z_LINES)
    result = jnp.sum(pieces.astype(f32), axis=0).astype(bf16)
    return result.reshape(STEPS, rows, SIZE)


def solution(mesh):
    placed = (
        P(None, "group", "tensor"),
        P(None, None, "tensor"),
        P("tensor", None),
        P("tensor"),
        P("tensor"),
        P("group", "tensor", None, None),
        P(),
        P(),
    )
    return jax.shard_map(
        body, mesh=mesh, in_specs=placed, out_specs=P(None, "group", "tensor"), check_vma=False
    )
```

```python
import functools

import jax
import jax.numpy as jnp
from jax import lax
from jax.experimental import pallas as pl
from jax.experimental.pallas import tpu as pltpu
from jax.sharding import PartitionSpec as P

STEPS = 4
SIZE = 128
MOVED = 13
XS, ZS, CORES = 4, 4, 2
CHIPS = XS * ZS
ZH, YS = 4, 4
SLOTS = 2
CODE = 64
PASSING = 5


def tensor_id(x, z, c):
    return (x * ZS + z) * CORES + c


SPOTS = [(x, z, c) for x in range(XS) for z in range(ZS) for c in range(CORES)]
Z_LINES = [[tensor_id(x, z, c) for z in range(ZS)] for x in range(XS) for c in range(CORES)]
X_RINGS = [[tensor_id(x, z, c) for x in range(XS)] for z in range(ZS) for c in range(CORES)]
X_CORES = [[tensor_id(x, z, c) for x in range(XS) for c in range(CORES)] for z in range(ZS)]
CORE_SWAP = [(tensor_id(x, z, c), tensor_id(x, z, 1 - c)) for x, z, c in SPOTS]
X_SHIFTS = [
    [(tensor_id(x, z, c), tensor_id((x + k) % XS, z, c)) for x, z, c in SPOTS] for k in range(XS)
]
Y_RINGS = [[z * YS + y for y in range(YS)] for z in range(ZH)]
Z_RINGS = [[z * YS + y for z in range(ZH)] for y in range(YS)]

VMEM = pl.BlockSpec(memory_space=pltpu.VMEM)
SMEM = pl.BlockSpec(memory_space=pltpu.SMEM)
ANY = pl.BlockSpec(memory_space=pl.ANY)
SMALL = pltpu.CompilerParams(vmem_limit_bytes=8 * 2**20)
ROOMY = pltpu.CompilerParams(vmem_limit_bytes=56 * 2**20)
DMA = pltpu.SemaphoreType.DMA


def after_kernel(x_ref, dep_ref, out_ref):
    pass


def after(x, dep):
    return pl.pallas_call(
        after_kernel,
        out_shape=jax.ShapeDtypeStruct(x.shape, x.dtype),
        in_specs=[ANY, ANY],
        out_specs=ANY,
        input_output_aliases={0: 0},
        name="after",
    )(x, dep)


def rows_on(migration_plan, own_group, groups, rows):
    plan = migration_plan.reshape(ZH, YS, rows)
    plan = lax.dynamic_index_in_dim(plan, own_group % YS, axis=1, keepdims=False)
    source = plan // rows
    target = jnp.arange(ZH) * YS + own_group % YS
    passing = (source // YS == own_group // YS) & (source != target[:, None])
    before = jnp.arange(rows)[None, :] < jnp.arange(rows)[:, None]
    order = jnp.sum((passing[:, None, :] & before).astype(jnp.int32), axis=-1)
    same = source[:, :, None] == source[:, None, :]
    slot = jnp.sum((same & (plan[:, None, :] < plan[:, :, None])).astype(jnp.int32), axis=-1)
    place = (source % YS) * (ZH * SLOTS) + jnp.arange(ZH)[:, None] * SLOTS + slot
    wanted = passing[:, None, :] & (order[:, None, :] == jnp.arange(PASSING)[None, :, None])
    place = jnp.sum(jnp.where(wanted, place[:, None, :], 0), axis=-1)
    return jnp.clip(place, 0, groups * SLOTS - 1).reshape(-1)


def pack_kernel(
    rows, plan_ref, states_ref, inputs_ref, out_ref, same_ref,
    wide_ref, narrow_ref, inputs_vmem, slot_ref, seen_ref, in_sem, out_sem, copy_sem,
):
    group = group_here()
    load = pltpu.make_async_copy(inputs_ref, inputs_vmem, copy_sem.at[0])
    load.start()
    for i in range(ZH * YS):
        seen_ref[i] = 0

    plan = plan_ref[...] - group * rows
    everyone = lax.broadcasted_iota(jnp.int32, plan.shape, 0) * plan.shape[1]
    everyone = everyone + lax.broadcasted_iota(jnp.int32, plan.shape, 1)
    everyone = everyone.astype(jnp.float32)
    targets = [jnp.max(jnp.where(plan == row, everyone, 0.0)).astype(jnp.int32) for row in range(rows)]
    count = jnp.int32(0)
    for row in range(rows):
        goal = lax.shift_right_logical(targets[row], rows.bit_length() - 1)
        leaves = (goal != group) & (count < MOVED)

        @pl.when(leaves)
        def _(row=row, goal=goal, count=count):
            rank = seen_ref[goal]
            seen_ref[goal] = rank + 1
            slot_ref[count] = (
                lax.rem(goal, YS) * (ZH * SLOTS) + lax.div(goal, YS) * SLOTS
                + jnp.minimum(rank, SLOTS - 1)
            )
            pltpu.make_async_copy(
                states_ref.at[row], wide_ref.at[count], in_sem.at[count]
            ).start()

        count = count + leaves.astype(jnp.int32)
    load.wait()
    store = pltpu.make_async_copy(inputs_vmem, same_ref, copy_sem.at[1])
    store.start()
    for i in range(MOVED):

        @pl.when(i < count)
        def _(i=i):
            pltpu.make_async_copy(states_ref.at[0], wide_ref.at[i], in_sem.at[i]).wait()
            narrow_ref[i] = wide_ref[i].astype(jnp.bfloat16)
            pltpu.make_async_copy(
                narrow_ref.at[i], out_ref.at[slot_ref[i]], out_sem.at[i]
            ).start()

    for i in range(MOVED):

        @pl.when(i < count)
        def _(i=i):
            pltpu.make_async_copy(narrow_ref.at[i], out_ref.at[0], out_sem.at[i]).wait()

    store.wait()


def pass_kernel(index_ref, rows_ref, dep_ref, out_ref, sem):
    copies = [
        pltpu.make_async_copy(rows_ref.at[index_ref[i]], out_ref.at[i], sem.at[i])
        for i in range(out_ref.shape[0])
    ]
    for copy in copies:
        copy.start()
    for copy in copies:
        copy.wait()


def group_here():
    return lax.axis_index("group")


def core_here():
    return lax.rem(lax.axis_index("tensor"), CORES)


def x_here():
    return lax.div(lax.axis_index("tensor"), CORES * ZS)


def columns(shift, z, core):
    spot = (lax.rem(x_here() + shift, XS) * ZS + z) * CORES + core
    return pl.ds(pl.multiple_of(spot * SIZE, SIZE), SIZE)


def lend_kernel(weight_ref, dep_ref, out_ref):
    other = 1 - core_here()
    for k in range(XS):
        for z in range(ZS):
            out_ref[k, z] = weight_ref[:, columns(k, z, other)]


def deal_kernel(weight_ref, lent_ref, *out_refs):
    core = core_here()
    for k in range(XS):
        for z in range(ZS):
            own, lent = weight_ref[:, columns(k, z, core)], lent_ref[k, z]
            out_refs[k][z, :SIZE] = jnp.where(core == 0, own, lent)
            out_refs[k][z, SIZE:] = jnp.where(core == 0, lent, own)


def split_rows(q):
    high = q.astype(jnp.bfloat16)
    low = (q - high.astype(jnp.float32)).astype(jnp.bfloat16)
    return jnp.concatenate([high, low], axis=0)


def project_kernel(
    rows, plan_ref, remaining_ref, decay_ref, gain_ref, own_ref, other_ref, weight_ref,
    states_ref, scaled_ref, partial_ref, gains_ref, code_ref, query_ref, kept_ref, active_ref,
    seen_ref,
):
    group, core = group_here(), core_here()
    count = STEPS * rows
    for i in range(ZH):
        seen_ref[i] = 0
    for i in range(code_ref.shape[0]):
        code_ref[i] = rows * CODE
    found = jnp.int32(0)
    for row in range(rows):
        source = plan_ref[group * rows + row]
        source_group = source // rows
        moved = (source_group != group) & (found < MOVED)
        far = source_group // YS
        rank = seen_ref[far]
        slot = far * PASSING + jnp.minimum(rank, PASSING - 1)
        step = moved.astype(jnp.int32)
        seen_ref[far] = rank + step
        code_ref[found] = jnp.where(moved, row * CODE + slot, rows * CODE)
        found = found + step
        active_ref[row : row + 1, :] = jnp.full((1, SIZE), remaining_ref[source], jnp.int32)
    acc = [jnp.zeros((count, SIZE), jnp.float32) for _ in range(3)]
    for chip in range(CHIPS):
        a, b = own_ref[chip], other_ref[chip]
        even = jnp.where(core == 0, a, b)
        odd = jnp.where(core == 0, b, a)
        both = jnp.concatenate([even, odd], axis=1)
        for i in range(3):
            weight = weight_ref[i, 2 * SIZE * chip : 2 * SIZE * (chip + 1), :]
            acc[i] += jnp.dot(both, weight, preferred_element_type=jnp.float32)
    query = acc[0] / (1.0 + jnp.exp(-acc[0]))
    key = acc[1] / (1.0 + jnp.exp(-acc[1]))
    value = acc[2]
    query_ref[...] = query
    for row in range(rows):
        source = plan_ref[group * rows + row]
        state = states_ref[source % rows]
        high = state.astype(jnp.bfloat16)
        low = (state - high.astype(jnp.float32)).astype(jnp.bfloat16)
        mine = query_ref[pl.ds(row, STEPS, stride=rows), :]
        pair = split_rows(mine)
        first = jnp.dot(pair, high, preferred_element_type=jnp.float32)
        second = jnp.dot(pair[:STEPS], low, preferred_element_type=jnp.float32)
        product = first[:STEPS] + first[STEPS:] + second
        stays = (source // rows == group).astype(jnp.float32)
        kept_ref[pl.ds(row, STEPS, stride=rows), :] = product * stays
    decay = decay_ref[0]
    at = lambda x, t: x[t * rows : (t + 1) * rows]
    power = decay
    for t in range(STEPS):
        here = slice(t * rows, (t + 1) * rows)
        scaled_ref[here] = power * at(query, t)
        readout = power * kept_ref[here]
        power = power * decay
        weight = jnp.float32(1.0)
        for s in range(t, -1, -1):
            score = jnp.sum(at(query, t) * at(key, s), axis=-1, keepdims=True)
            readout = readout + (weight * score) * at(value, s)
            weight = weight * decay
        partial_ref[here] = readout
        gains_ref[here] = jnp.where(active_ref[...] > t, gain_ref[...], 0.0)


def finish_kernel(
    rows, code_ref, scaled_ref, partial_ref, gains_ref, incoming_ref, normed_ref, moved_ref
):
    room = moved_ref.shape[0] // STEPS
    moved_ref[...] = jnp.zeros_like(moved_ref)
    for i in range(MOVED):
        row = lax.div(code_ref[i], CODE)
        mine = scaled_ref[pl.ds(jnp.minimum(row, rows - 1), STEPS, stride=rows), :]
        state = incoming_ref[lax.rem(code_ref[i], CODE)]
        product = jnp.dot(split_rows(mine), state, preferred_element_type=jnp.float32)
        moved_ref[pl.ds(row, STEPS, stride=room), :] = product[:STEPS] + product[STEPS:]
    for t in range(STEPS):
        here = slice(t * rows, (t + 1) * rows)
        readout = partial_ref[here] + moved_ref[t * room : t * room + rows]
        norm = lax.rsqrt(jnp.mean(readout * readout, axis=-1, keepdims=True) + 1e-05)
        normed_ref[here] = (readout * norm * gains_ref[here]).astype(jnp.bfloat16)


def output_kernel(ring_ref, *refs):
    weights, out_ref = refs[:XS], refs[XS]
    x = x_here()
    sources = [lax.rem(x + XS - k, XS) * CORES for k in range(XS)]
    rows = [
        jnp.concatenate([ring_ref[source + c] for c in range(CORES)], axis=1) for source in sources
    ]
    for z in range(ZS):
        total = 0.0
        for k in range(XS):
            total = total + jnp.dot(rows[k], weights[k][z], preferred_element_type=jnp.float32)
        out_ref[z] = total.astype(jnp.bfloat16)


def body(
    step_inputs,
    qkv_weight,
    out_weight,
    head_gain,
    head_decay,
    states_in,
    remaining_steps,
    migration_plan,
):
    rows = states_in.shape[0]
    count = STEPS * rows
    groups = lax.axis_size("group")
    own_group = lax.axis_index("group")
    states = states_in.reshape(rows, SIZE, SIZE)
    bf16, f32 = jnp.bfloat16, jnp.float32

    outgoing, inputs = pl.pallas_call(
        functools.partial(pack_kernel, rows),
        out_shape=[
            jax.ShapeDtypeStruct((groups * SLOTS, SIZE, SIZE), bf16),
            jax.ShapeDtypeStruct((count, SIZE), bf16),
        ],
        in_specs=[VMEM, ANY, ANY],
        out_specs=[ANY, ANY],
        scratch_shapes=[
            pltpu.VMEM((MOVED, SIZE, SIZE), f32),
            pltpu.VMEM((MOVED, SIZE, SIZE), bf16),
            pltpu.VMEM((count, SIZE), bf16),
            pltpu.SMEM((MOVED,), jnp.int32),
            pltpu.SMEM((ZH * YS,), jnp.int32),
            DMA((MOVED,)),
            DMA((MOVED,)),
            DMA((2,)),
        ],
        compiler_params=ROOMY,
        name="pack",
    )(migration_plan.reshape(ZH, YS * rows), states, step_inputs.reshape(count, SIZE))
    passing = lax.all_to_all(outgoing, "group", 0, 0, tiled=True, axis_index_groups=Y_RINGS)
    line = lax.all_gather(inputs, "tensor", axis=0, axis_index_groups=Z_LINES)
    passing = pl.pallas_call(
        pass_kernel,
        out_shape=jax.ShapeDtypeStruct((ZH * PASSING, SIZE, SIZE), bf16),
        in_specs=[SMEM, VMEM, VMEM],
        out_specs=ANY,
        scratch_shapes=[DMA((ZH * PASSING,))],
        compiler_params=SMALL,
        name="pass_on",
    )(rows_on(migration_plan, own_group, groups, rows), passing, line)
    incoming = lax.all_to_all(passing, "group", 0, 0, tiled=True, axis_index_groups=Z_RINGS)

    plane = lax.all_gather(after(line, passing), "tensor", axis=0, axis_index_groups=X_RINGS)
    plane = plane.reshape(CHIPS, count, SIZE)
    other = lax.ppermute(plane, "tensor", CORE_SWAP)
    scaled, partial, gains, code = pl.pallas_call(
        functools.partial(project_kernel, rows),
        out_shape=[
            jax.ShapeDtypeStruct((count, SIZE), f32),
            jax.ShapeDtypeStruct((count, SIZE), f32),
            jax.ShapeDtypeStruct((count, SIZE), f32),
            jax.ShapeDtypeStruct((MOVED + 1,), jnp.int32),
        ],
        in_specs=[SMEM, SMEM, SMEM, VMEM, VMEM, VMEM, VMEM, VMEM],
        out_specs=[VMEM, VMEM, VMEM, SMEM],
        scratch_shapes=[
            pltpu.VMEM((count, SIZE), f32),
            pltpu.VMEM((count, SIZE), f32),
            pltpu.VMEM((rows, SIZE), jnp.int32),
            pltpu.SMEM((ZH,), jnp.int32),
        ],
        compiler_params=pltpu.CompilerParams(vmem_limit_bytes=16 * 2**20),
        cost_estimate=pl.CostEstimate(
            flops=2 * count * 4096 * 384, bytes_accessed=6 * 2**20, transcendentals=0
        ),
        name="project",
    )(
        migration_plan, remaining_steps, head_decay, head_gain.reshape(1, SIZE), plane, other,
        jnp.transpose(qkv_weight, (1, 0, 2)), states,
    )

    lent = pl.pallas_call(
        lend_kernel,
        out_shape=jax.ShapeDtypeStruct((XS, ZS, SIZE, SIZE), bf16),
        in_specs=[VMEM, ANY],
        out_specs=VMEM,
        compiler_params=SMALL,
        name="lend",
    )(out_weight, passing)
    lent = lax.ppermute(lent, "tensor", CORE_SWAP)
    dealt = pl.pallas_call(
        deal_kernel,
        out_shape=[jax.ShapeDtypeStruct((ZS, CORES * SIZE, SIZE), bf16)] * XS,
        in_specs=[VMEM, VMEM],
        out_specs=[VMEM] * XS,
        compiler_params=SMALL,
        name="deal",
    )(out_weight, lent)
    dealt = [dealt[0]] + [lax.ppermute(dealt[k], "tensor", X_SHIFTS[k]) for k in range(1, XS)]

    normed = pl.pallas_call(
        functools.partial(finish_kernel, rows),
        out_shape=jax.ShapeDtypeStruct((count, SIZE), bf16),
        in_specs=[SMEM, VMEM, VMEM, VMEM, VMEM],
        out_specs=VMEM,
        scratch_shapes=[pltpu.VMEM((STEPS * (rows + 8), SIZE), f32)],
        compiler_params=SMALL,
        name="finish",
    )(code, scaled, partial, gains, incoming)
    ring = lax.all_gather(normed, "tensor", axis=0, axis_index_groups=X_CORES)
    sums = pl.pallas_call(
        output_kernel,
        out_shape=jax.ShapeDtypeStruct((ZS, count, SIZE), bf16),
        in_specs=[VMEM] * (1 + XS),
        out_specs=VMEM,
        compiler_params=SMALL,
        name="output",
    )(ring, *dealt)
    pieces = lax.all_to_all(sums, "tensor", 0, 0, tiled=True, axis_index_groups=Z_LINES)
    result = jnp.sum(pieces.astype(f32), axis=0).astype(bf16)
    return result.reshape(STEPS, rows, SIZE)


def solution(mesh):
    placed = (
        P(None, "group", "tensor"),
        P(None, None, "tensor"),
        P("tensor", None),
        P("tensor"),
        P("tensor"),
        P("group", "tensor", None, None),
        P(),
        P(),
    )
    return jax.shard_map(
        body, mesh=mesh, in_specs=placed, out_specs=P(None, "group", "tensor"), check_vma=False
    )
```

```python
import functools

import jax
import jax.numpy as jnp
from jax import lax
from jax.experimental import pallas as pl
from jax.experimental.pallas import tpu as pltpu
from jax.sharding import PartitionSpec as P

STEPS = 4
SIZE = 128
MOVED = 13
XS, ZS, CORES = 4, 4, 2
CHIPS = XS * ZS
ZH, YS = 4, 4
SLOTS = 2
CODE = 64
PASSING = 5


def tensor_id(x, z, c):
    return (x * ZS + z) * CORES + c


SPOTS = [(x, z, c) for x in range(XS) for z in range(ZS) for c in range(CORES)]
Z_LINES = [[tensor_id(x, z, c) for z in range(ZS)] for x in range(XS) for c in range(CORES)]
X_RINGS = [[tensor_id(x, z, c) for x in range(XS)] for z in range(ZS) for c in range(CORES)]
X_CORES = [[tensor_id(x, z, c) for x in range(XS) for c in range(CORES)] for z in range(ZS)]
CORE_SWAP = [(tensor_id(x, z, c), tensor_id(x, z, 1 - c)) for x, z, c in SPOTS]
X_SHIFTS = [
    [(tensor_id(x, z, c), tensor_id((x + k) % XS, z, c)) for x, z, c in SPOTS] for k in range(XS)
]
Y_RINGS = [[z * YS + y for y in range(YS)] for z in range(ZH)]
Z_RINGS = [[z * YS + y for z in range(ZH)] for y in range(YS)]

VMEM = pl.BlockSpec(memory_space=pltpu.VMEM)
SMEM = pl.BlockSpec(memory_space=pltpu.SMEM)
ANY = pl.BlockSpec(memory_space=pl.ANY)
SMALL = pltpu.CompilerParams(vmem_limit_bytes=8 * 2**20)
ROOMY = pltpu.CompilerParams(vmem_limit_bytes=56 * 2**20)
DMA = pltpu.SemaphoreType.DMA


def after_kernel(x_ref, dep_ref, out_ref):
    pass


def after(x, dep):
    return pl.pallas_call(
        after_kernel,
        out_shape=jax.ShapeDtypeStruct(x.shape, x.dtype),
        in_specs=[ANY, ANY],
        out_specs=ANY,
        input_output_aliases={0: 0},
        name="after",
    )(x, dep)


def rows_on(migration_plan, own_group, groups, rows):
    plan = migration_plan.reshape(ZH, YS, rows)
    plan = lax.dynamic_index_in_dim(plan, own_group % YS, axis=1, keepdims=False)
    source = plan // rows
    target = jnp.arange(ZH) * YS + own_group % YS
    passing = (source // YS == own_group // YS) & (source != target[:, None])
    before = jnp.arange(rows)[None, :] < jnp.arange(rows)[:, None]
    order = jnp.sum((passing[:, None, :] & before).astype(jnp.int32), axis=-1)
    same = source[:, :, None] == source[:, None, :]
    slot = jnp.sum((same & (plan[:, None, :] < plan[:, :, None])).astype(jnp.int32), axis=-1)
    place = (source % YS) * (ZH * SLOTS) + jnp.arange(ZH)[:, None] * SLOTS + slot
    wanted = passing[:, None, :] & (order[:, None, :] == jnp.arange(PASSING)[None, :, None])
    place = jnp.sum(jnp.where(wanted, place[:, None, :], 0), axis=-1)
    return jnp.clip(place, 0, groups * SLOTS - 1).reshape(-1)


def pack_kernel(
    rows, plan_hbm, states_hbm, inputs_hbm, out_ref, same_ref,
    plan_ref, states_ref, inputs_ref, narrow_ref, seen_ref, in_sem, out_sem,
):
    group = group_here()
    loads = [
        pltpu.make_async_copy(plan_hbm, plan_ref, in_sem.at[0]),
        pltpu.make_async_copy(inputs_hbm, inputs_ref, in_sem.at[1]),
        pltpu.make_async_copy(states_hbm, states_ref, in_sem.at[2]),
    ]
    for load in loads:
        load.start()
    for i in range(ZH * YS):
        seen_ref[i] = 0
    loads[0].wait()
    plan = plan_ref[...] - group * rows
    everyone = lax.broadcasted_iota(jnp.int32, plan.shape, 0) * plan.shape[1]
    everyone = everyone + lax.broadcasted_iota(jnp.int32, plan.shape, 1)
    everyone = everyone.astype(jnp.float32)
    targets = [
        jnp.max(jnp.where(plan == row, everyone, 0.0)).astype(jnp.int32) for row in range(rows)
    ]
    loads[1].wait()
    store = pltpu.make_async_copy(inputs_ref, same_ref, out_sem.at[MOVED])
    store.start()
    loads[2].wait()
    count = jnp.int32(0)
    for row in range(rows):
        goal = lax.shift_right_logical(targets[row], rows.bit_length() - 1)
        leaves = (goal != group) & (count < MOVED)

        @pl.when(leaves)
        def _(row=row, goal=goal, count=count):
            rank = seen_ref[goal]
            seen_ref[goal] = rank + 1
            slot = (
                lax.rem(goal, YS) * (ZH * SLOTS) + lax.div(goal, YS) * SLOTS
                + jnp.minimum(rank, SLOTS - 1)
            )
            narrow_ref[count] = states_ref[row].astype(jnp.bfloat16)
            pltpu.make_async_copy(
                narrow_ref.at[count], out_ref.at[slot], out_sem.at[count]
            ).start()

        count = count + leaves.astype(jnp.int32)
    for i in range(MOVED):

        @pl.when(i < count)
        def _(i=i):
            pltpu.make_async_copy(narrow_ref.at[i], out_ref.at[0], out_sem.at[i]).wait()

    store.wait()


def pass_kernel(index_ref, rows_ref, dep_ref, out_ref, held_ref, sem):
    copies = []
    for z in range(ZH):
        part = pl.ds(z * PASSING, PASSING)
        for i in range(z * PASSING, (z + 1) * PASSING):
            held_ref[i] = rows_ref[index_ref[i]]
        copies.append(pltpu.make_async_copy(held_ref.at[part], out_ref.at[part], sem.at[z]))
        copies[z].start()
    for copy in copies:
        copy.wait()


def group_here():
    return lax.axis_index("group")


def core_here():
    return lax.rem(lax.axis_index("tensor"), CORES)


def x_here():
    return lax.div(lax.axis_index("tensor"), CORES * ZS)


def columns(shift, z, core):
    spot = (lax.rem(x_here() + shift, XS) * ZS + z) * CORES + core
    return pl.ds(pl.multiple_of(spot * SIZE, SIZE), SIZE)


def lend_kernel(weight_ref, dep_ref, out_ref):
    other = 1 - core_here()
    for k in range(XS):
        for z in range(ZS):
            out_ref[k, z] = weight_ref[:, columns(k, z, other)]


def deal_kernel(weight_ref, lent_ref, *out_refs):
    core = core_here()
    for k in range(XS):
        for z in range(ZS):
            own, lent = weight_ref[:, columns(k, z, core)], lent_ref[k, z]
            out_refs[k][z, :SIZE] = jnp.where(core == 0, own, lent)
            out_refs[k][z, SIZE:] = jnp.where(core == 0, lent, own)


def split_rows(q):
    high = q.astype(jnp.bfloat16)
    low = (q - high.astype(jnp.float32)).astype(jnp.bfloat16)
    return jnp.concatenate([high, low], axis=0)


def project_kernel(
    rows, plan_ref, remaining_ref, decay_ref, gain_ref, own_ref, other_ref, weight_ref,
    states_ref, scaled_ref, partial_ref, gains_ref, code_ref, query_ref, kept_ref, active_ref,
    seen_ref,
):
    group, core = group_here(), core_here()
    count = STEPS * rows
    for i in range(ZH):
        seen_ref[i] = 0
    for i in range(code_ref.shape[0]):
        code_ref[i] = rows * CODE
    found = jnp.int32(0)
    for row in range(rows):
        source = plan_ref[group * rows + row]
        source_group = source // rows
        moved = (source_group != group) & (found < MOVED)
        far = source_group // YS
        rank = seen_ref[far]
        slot = far * PASSING + jnp.minimum(rank, PASSING - 1)
        step = moved.astype(jnp.int32)
        seen_ref[far] = rank + step
        code_ref[found] = jnp.where(moved, row * CODE + slot, rows * CODE)
        found = found + step
        active_ref[row : row + 1, :] = jnp.full((1, SIZE), remaining_ref[source], jnp.int32)
    acc = [jnp.zeros((count, SIZE), jnp.float32) for _ in range(3)]
    for chip in range(CHIPS):
        a, b = own_ref[chip], other_ref[chip]
        even = jnp.where(core == 0, a, b)
        odd = jnp.where(core == 0, b, a)
        both = jnp.concatenate([even, odd], axis=1)
        for i in range(3):
            weight = weight_ref[i, 2 * SIZE * chip : 2 * SIZE * (chip + 1), :]
            acc[i] += jnp.dot(both, weight, preferred_element_type=jnp.float32)
    query = acc[0] / (1.0 + jnp.exp(-acc[0]))
    key = acc[1] / (1.0 + jnp.exp(-acc[1]))
    value = acc[2]
    query_ref[...] = query
    for row in range(rows):
        source = plan_ref[group * rows + row]
        state = states_ref[source % rows]
        high = state.astype(jnp.bfloat16)
        low = (state - high.astype(jnp.float32)).astype(jnp.bfloat16)
        mine = query_ref[pl.ds(row, STEPS, stride=rows), :]
        pair = split_rows(mine)
        first = jnp.dot(pair, high, preferred_element_type=jnp.float32)
        second = jnp.dot(pair[:STEPS], low, preferred_element_type=jnp.float32)
        product = first[:STEPS] + first[STEPS:] + second
        stays = (source // rows == group).astype(jnp.float32)
        kept_ref[pl.ds(row, STEPS, stride=rows), :] = product * stays
    decay = decay_ref[0]
    at = lambda x, t: x[t * rows : (t + 1) * rows]
    power = decay
    for t in range(STEPS):
        here = slice(t * rows, (t + 1) * rows)
        scaled_ref[here] = power * at(query, t)
        readout = power * kept_ref[here]
        power = power * decay
        weight = jnp.float32(1.0)
        for s in range(t, -1, -1):
            score = jnp.sum(at(query, t) * at(key, s), axis=-1, keepdims=True)
            readout = readout + (weight * score) * at(value, s)
            weight = weight * decay
        partial_ref[here] = readout
        gains_ref[here] = jnp.where(active_ref[...] > t, gain_ref[...], 0.0)


def finish_kernel(
    rows, code_ref, scaled_ref, partial_ref, gains_ref, incoming_ref, normed_ref, moved_ref
):
    room = moved_ref.shape[0] // STEPS
    moved_ref[...] = jnp.zeros_like(moved_ref)
    for i in range(MOVED):
        row = lax.div(code_ref[i], CODE)
        mine = scaled_ref[pl.ds(jnp.minimum(row, rows - 1), STEPS, stride=rows), :]
        state = incoming_ref[lax.rem(code_ref[i], CODE)]
        product = jnp.dot(split_rows(mine), state, preferred_element_type=jnp.float32)
        moved_ref[pl.ds(row, STEPS, stride=room), :] = product[:STEPS] + product[STEPS:]
    for t in range(STEPS):
        here = slice(t * rows, (t + 1) * rows)
        readout = partial_ref[here] + moved_ref[t * room : t * room + rows]
        norm = lax.rsqrt(jnp.mean(readout * readout, axis=-1, keepdims=True) + 1e-05)
        normed_ref[here] = (readout * norm * gains_ref[here]).astype(jnp.bfloat16)


def output_kernel(ring_ref, *refs):
    weights, out_ref = refs[:XS], refs[XS]
    x = x_here()
    sources = [lax.rem(x + XS - k, XS) * CORES for k in range(XS)]
    rows = [
        jnp.concatenate([ring_ref[source + c] for c in range(CORES)], axis=1) for source in sources
    ]
    for z in range(ZS):
        total = 0.0
        for k in range(XS):
            total = total + jnp.dot(rows[k], weights[k][z], preferred_element_type=jnp.float32)
        out_ref[z] = total.astype(jnp.bfloat16)


def body(
    step_inputs,
    qkv_weight,
    out_weight,
    head_gain,
    head_decay,
    states_in,
    remaining_steps,
    migration_plan,
):
    rows = states_in.shape[0]
    count = STEPS * rows
    groups = lax.axis_size("group")
    own_group = lax.axis_index("group")
    states = states_in.reshape(rows, SIZE, SIZE)
    bf16, f32 = jnp.bfloat16, jnp.float32

    outgoing, inputs = pl.pallas_call(
        functools.partial(pack_kernel, rows),
        out_shape=[
            jax.ShapeDtypeStruct((groups * SLOTS, SIZE, SIZE), bf16),
            jax.ShapeDtypeStruct((count, SIZE), bf16),
        ],
        in_specs=[ANY, ANY, ANY],
        out_specs=[ANY, ANY],
        scratch_shapes=[
            pltpu.VMEM((ZH, YS * rows), jnp.int32),
            pltpu.VMEM((rows, SIZE, SIZE), f32),
            pltpu.VMEM((count, SIZE), bf16),
            pltpu.VMEM((MOVED, SIZE, SIZE), bf16),
            pltpu.SMEM((ZH * YS,), jnp.int32),
            DMA((3,)),
            DMA((MOVED + 1,)),
        ],
        compiler_params=ROOMY,
        name="pack",
    )(migration_plan.reshape(ZH, YS * rows), states, step_inputs.reshape(count, SIZE))
    passing = lax.all_to_all(outgoing, "group", 0, 0, tiled=True, axis_index_groups=Y_RINGS)
    line = lax.all_gather(inputs, "tensor", axis=0, axis_index_groups=Z_LINES)
    passing = pl.pallas_call(
        pass_kernel,
        out_shape=jax.ShapeDtypeStruct((ZH * PASSING, SIZE, SIZE), bf16),
        in_specs=[SMEM, VMEM, VMEM],
        out_specs=ANY,
        scratch_shapes=[pltpu.VMEM((ZH * PASSING, SIZE, SIZE), bf16), DMA((ZH,))],
        compiler_params=SMALL,
        name="pass_on",
    )(rows_on(migration_plan, own_group, groups, rows), passing, line)
    incoming = lax.all_to_all(passing, "group", 0, 0, tiled=True, axis_index_groups=Z_RINGS)

    plane = lax.all_gather(after(line, passing), "tensor", axis=0, axis_index_groups=X_RINGS)
    plane = plane.reshape(CHIPS, count, SIZE)
    other = lax.ppermute(plane, "tensor", CORE_SWAP)
    scaled, partial, gains, code = pl.pallas_call(
        functools.partial(project_kernel, rows),
        out_shape=[
            jax.ShapeDtypeStruct((count, SIZE), f32),
            jax.ShapeDtypeStruct((count, SIZE), f32),
            jax.ShapeDtypeStruct((count, SIZE), f32),
            jax.ShapeDtypeStruct((MOVED + 1,), jnp.int32),
        ],
        in_specs=[SMEM, SMEM, SMEM, VMEM, VMEM, VMEM, VMEM, VMEM],
        out_specs=[VMEM, VMEM, VMEM, SMEM],
        scratch_shapes=[
            pltpu.VMEM((count, SIZE), f32),
            pltpu.VMEM((count, SIZE), f32),
            pltpu.VMEM((rows, SIZE), jnp.int32),
            pltpu.SMEM((ZH,), jnp.int32),
        ],
        compiler_params=pltpu.CompilerParams(vmem_limit_bytes=16 * 2**20),
        cost_estimate=pl.CostEstimate(
            flops=2 * count * 4096 * 384, bytes_accessed=6 * 2**20, transcendentals=0
        ),
        name="project",
    )(
        migration_plan, remaining_steps, head_decay, head_gain.reshape(1, SIZE), plane, other,
        jnp.transpose(qkv_weight, (1, 0, 2)), states,
    )

    lent = pl.pallas_call(
        lend_kernel,
        out_shape=jax.ShapeDtypeStruct((XS, ZS, SIZE, SIZE), bf16),
        in_specs=[VMEM, ANY],
        out_specs=VMEM,
        compiler_params=SMALL,
        name="lend",
    )(out_weight, passing)
    lent = lax.ppermute(lent, "tensor", CORE_SWAP)
    dealt = pl.pallas_call(
        deal_kernel,
        out_shape=[jax.ShapeDtypeStruct((ZS, CORES * SIZE, SIZE), bf16)] * XS,
        in_specs=[VMEM, VMEM],
        out_specs=[VMEM] * XS,
        compiler_params=SMALL,
        name="deal",
    )(out_weight, lent)
    dealt = [dealt[0]] + [lax.ppermute(dealt[k], "tensor", X_SHIFTS[k]) for k in range(1, XS)]

    normed = pl.pallas_call(
        functools.partial(finish_kernel, rows),
        out_shape=jax.ShapeDtypeStruct((count, SIZE), bf16),
        in_specs=[SMEM, VMEM, VMEM, VMEM, VMEM],
        out_specs=VMEM,
        scratch_shapes=[pltpu.VMEM((STEPS * (rows + 8), SIZE), f32)],
        compiler_params=SMALL,
        name="finish",
    )(code, scaled, partial, gains, incoming)
    ring = lax.all_gather(normed, "tensor", axis=0, axis_index_groups=X_CORES)
    sums = pl.pallas_call(
        output_kernel,
        out_shape=jax.ShapeDtypeStruct((ZS, count, SIZE), bf16),
        in_specs=[VMEM] * (1 + XS),
        out_specs=VMEM,
        compiler_params=SMALL,
        name="output",
    )(ring, *dealt)
    pieces = lax.all_to_all(sums, "tensor", 0, 0, tiled=True, axis_index_groups=Z_LINES)
    result = jnp.sum(pieces.astype(f32), axis=0).astype(bf16)
    return result.reshape(STEPS, rows, SIZE)


def solution(mesh):
    placed = (
        P(None, "group", "tensor"),
        P(None, None, "tensor"),
        P("tensor", None),
        P("tensor"),
        P("tensor"),
        P("group", "tensor", None, None),
        P(),
        P(),
    )
    return jax.shard_map(
        body, mesh=mesh, in_specs=placed, out_specs=P(None, "group", "tensor"), check_vma=False
    )
```

```python
import functools

import jax
import jax.numpy as jnp
from jax import lax
from jax.experimental import pallas as pl
from jax.experimental.pallas import tpu as pltpu
from jax.sharding import PartitionSpec as P

STEPS = 4
SIZE = 128
MOVED = 13
XS, ZS, CORES = 4, 4, 2
CHIPS = XS * ZS
ZH, YS = 4, 4
SLOTS = 2
CODE = 64
PASSING = 5


def tensor_id(x, z, c):
    return (x * ZS + z) * CORES + c


SPOTS = [(x, z, c) for x in range(XS) for z in range(ZS) for c in range(CORES)]
Z_LINES = [[tensor_id(x, z, c) for z in range(ZS)] for x in range(XS) for c in range(CORES)]
X_RINGS = [[tensor_id(x, z, c) for x in range(XS)] for z in range(ZS) for c in range(CORES)]
X_CORES = [[tensor_id(x, z, c) for x in range(XS) for c in range(CORES)] for z in range(ZS)]
CORE_SWAP = [(tensor_id(x, z, c), tensor_id(x, z, 1 - c)) for x, z, c in SPOTS]
X_SHIFTS = [
    [(tensor_id(x, z, c), tensor_id((x + k) % XS, z, c)) for x, z, c in SPOTS] for k in range(XS)
]
Y_RINGS = [[z * YS + y for y in range(YS)] for z in range(ZH)]
Z_RINGS = [[z * YS + y for z in range(ZH)] for y in range(YS)]

VMEM = pl.BlockSpec(memory_space=pltpu.VMEM)
SMEM = pl.BlockSpec(memory_space=pltpu.SMEM)
ANY = pl.BlockSpec(memory_space=pl.ANY)
SMALL = pltpu.CompilerParams(vmem_limit_bytes=8 * 2**20)
ROOMY = pltpu.CompilerParams(vmem_limit_bytes=56 * 2**20)
DMA = pltpu.SemaphoreType.DMA


def after_kernel(x_ref, dep_ref, out_ref):
    pass


def after(x, dep):
    return pl.pallas_call(
        after_kernel,
        out_shape=jax.ShapeDtypeStruct(x.shape, x.dtype),
        in_specs=[ANY, ANY],
        out_specs=ANY,
        input_output_aliases={0: 0},
        name="after",
    )(x, dep)


def rows_on(migration_plan, own_group, groups, rows):
    plan = migration_plan.reshape(ZH, YS, rows)
    plan = lax.dynamic_index_in_dim(plan, own_group % YS, axis=1, keepdims=False)
    source = plan // rows
    target = jnp.arange(ZH) * YS + own_group % YS
    passing = (source // YS == own_group // YS) & (source != target[:, None])
    before = jnp.arange(rows)[None, :] < jnp.arange(rows)[:, None]
    order = jnp.sum((passing[:, None, :] & before).astype(jnp.int32), axis=-1)
    same = source[:, :, None] == source[:, None, :]
    slot = jnp.sum((same & (plan[:, None, :] < plan[:, :, None])).astype(jnp.int32), axis=-1)
    place = (source % YS) * (ZH * SLOTS) + jnp.arange(ZH)[:, None] * SLOTS + slot
    wanted = passing[:, None, :] & (order[:, None, :] == jnp.arange(PASSING)[None, :, None])
    place = jnp.sum(jnp.where(wanted, place[:, None, :], 0), axis=-1)
    return jnp.clip(place, 0, groups * SLOTS - 1).reshape(-1)


def pack_kernel(
    rows, plan_hbm, states_hbm, inputs_hbm, out_ref, same_ref,
    plan_ref, states_ref, inputs_ref, narrow_ref, seen_ref, in_sem, out_sem,
):
    group = group_here()
    loads = [
        pltpu.make_async_copy(plan_hbm, plan_ref, in_sem.at[0]),
        pltpu.make_async_copy(inputs_hbm, inputs_ref, in_sem.at[1]),
        pltpu.make_async_copy(states_hbm, states_ref, in_sem.at[2]),
    ]
    for load in loads:
        load.start()
    for i in range(ZH * YS):
        seen_ref[i] = 0
    loads[0].wait()
    plan = plan_ref[...] - group * rows
    everyone = lax.broadcasted_iota(jnp.int32, plan.shape, 0) * plan.shape[1]
    everyone = everyone + lax.broadcasted_iota(jnp.int32, plan.shape, 1)
    everyone = everyone.astype(jnp.float32)
    targets = [
        jnp.max(jnp.where(plan == row, everyone, 0.0)).astype(jnp.int32) for row in range(rows)
    ]
    loads[1].wait()
    store = pltpu.make_async_copy(inputs_ref, same_ref, out_sem.at[MOVED])
    store.start()
    loads[2].wait()
    count = jnp.int32(0)
    for row in range(rows):
        goal = lax.shift_right_logical(targets[row], rows.bit_length() - 1)
        leaves = (goal != group) & (count < MOVED)

        @pl.when(leaves)
        def _(row=row, goal=goal, count=count):
            rank = seen_ref[goal]
            seen_ref[goal] = rank + 1
            slot = (
                lax.rem(goal, YS) * (ZH * SLOTS) + lax.div(goal, YS) * SLOTS
                + jnp.minimum(rank, SLOTS - 1)
            )
            narrow_ref[count] = states_ref[row].astype(jnp.bfloat16)
            pltpu.make_async_copy(
                narrow_ref.at[count], out_ref.at[slot], out_sem.at[count]
            ).start()

        count = count + leaves.astype(jnp.int32)
    for i in range(MOVED):

        @pl.when(i < count)
        def _(i=i):
            pltpu.make_async_copy(narrow_ref.at[i], out_ref.at[0], out_sem.at[i]).wait()

    store.wait()


def pass_kernel(index_ref, rows_ref, dep_ref, out_ref, held_ref, sem):
    copies = []
    for z in range(ZH):
        part = pl.ds(z * PASSING, PASSING)
        for i in range(z * PASSING, (z + 1) * PASSING):
            held_ref[i] = rows_ref[index_ref[i]]
        copies.append(pltpu.make_async_copy(held_ref.at[part], out_ref.at[part], sem.at[z]))
        copies[z].start()
    for copy in copies:
        copy.wait()


def group_here():
    return lax.axis_index("group")


def core_here():
    return lax.rem(lax.axis_index("tensor"), CORES)


def x_here():
    return lax.div(lax.axis_index("tensor"), CORES * ZS)


def columns(shift, z, core):
    spot = (lax.rem(x_here() + shift, XS) * ZS + z) * CORES + core
    return pl.ds(pl.multiple_of(spot * SIZE, SIZE), SIZE)


def lend_kernel(weight_ref, dep_ref, out_ref):
    other = 1 - core_here()
    for k in range(XS):
        for z in range(ZS):
            out_ref[k, z] = weight_ref[:, columns(k, z, other)]


def deal_kernel(weight_ref, lent_ref, *out_refs):
    core = core_here()
    for k in range(XS):
        for z in range(ZS):
            own, lent = weight_ref[:, columns(k, z, core)], lent_ref[k, z]
            out_refs[k][z, :SIZE] = jnp.where(core == 0, own, lent)
            out_refs[k][z, SIZE:] = jnp.where(core == 0, lent, own)


def split_rows(q):
    high = q.astype(jnp.bfloat16)
    low = (q - high.astype(jnp.float32)).astype(jnp.bfloat16)
    return jnp.concatenate([high, low], axis=0)


def project_kernel(
    rows, plan_ref, remaining_ref, decay_ref, gain_ref, own_ref, other_ref, weight_ref,
    states_ref, scaled_ref, partial_ref, gains_ref, code_ref, query_ref, kept_ref, active_ref,
    seen_ref,
):
    group, core = group_here(), core_here()
    count = STEPS * rows
    for i in range(ZH):
        seen_ref[i] = 0
    for i in range(code_ref.shape[0]):
        code_ref[i] = rows * CODE
    found = jnp.int32(0)
    for row in range(rows):
        source = plan_ref[group * rows + row]
        source_group = source // rows
        moved = (source_group != group) & (found < MOVED)
        far = source_group // YS
        rank = seen_ref[far]
        slot = far * PASSING + jnp.minimum(rank, PASSING - 1)
        step = moved.astype(jnp.int32)
        seen_ref[far] = rank + step
        code_ref[found] = jnp.where(moved, row * CODE + slot, rows * CODE)
        found = found + step
        active_ref[row : row + 1, :] = jnp.full((1, SIZE), remaining_ref[source], jnp.int32)
    acc = [jnp.zeros((count, SIZE), jnp.float32) for _ in range(3)]
    for chip in range(CHIPS):
        a, b = own_ref[chip], other_ref[chip]
        even = jnp.where(core == 0, a, b)
        odd = jnp.where(core == 0, b, a)
        both = jnp.concatenate([even, odd], axis=1)
        for i in range(3):
            weight = weight_ref[i, 2 * SIZE * chip : 2 * SIZE * (chip + 1), :]
            acc[i] += jnp.dot(both, weight, preferred_element_type=jnp.float32)
    query = acc[0] / (1.0 + jnp.exp(-acc[0]))
    key = acc[1] / (1.0 + jnp.exp(-acc[1]))
    value = acc[2]
    query_ref[...] = query
    for row in range(rows):
        source = plan_ref[group * rows + row]
        state = states_ref[source % rows]
        high = state.astype(jnp.bfloat16)
        low = (state - high.astype(jnp.float32)).astype(jnp.bfloat16)
        mine = query_ref[pl.ds(row, STEPS, stride=rows), :]
        pair = split_rows(mine)
        first = jnp.dot(pair, high, preferred_element_type=jnp.float32)
        second = jnp.dot(pair[:STEPS], low, preferred_element_type=jnp.float32)
        product = first[:STEPS] + first[STEPS:] + second
        stays = (source // rows == group).astype(jnp.float32)
        kept_ref[pl.ds(row, STEPS, stride=rows), :] = product * stays
    decay = decay_ref[0]
    at = lambda x, t: x[t * rows : (t + 1) * rows]
    power = decay
    for t in range(STEPS):
        here = slice(t * rows, (t + 1) * rows)
        scaled_ref[here] = power * at(query, t)
        readout = power * kept_ref[here]
        power = power * decay
        weight = jnp.float32(1.0)
        for s in range(t, -1, -1):
            score = jnp.sum(at(query, t) * at(key, s), axis=-1, keepdims=True)
            readout = readout + (weight * score) * at(value, s)
            weight = weight * decay
        partial_ref[here] = readout
        gains_ref[here] = jnp.where(active_ref[...] > t, gain_ref[...], 0.0)


def finish_kernel(
    rows, code_ref, scaled_ref, partial_ref, gains_ref, incoming_ref, normed_ref, moved_ref
):
    room = moved_ref.shape[0] // STEPS
    moved_ref[...] = jnp.zeros_like(moved_ref)
    for i in range(MOVED):
        row = lax.div(code_ref[i], CODE)
        mine = scaled_ref[pl.ds(jnp.minimum(row, rows - 1), STEPS, stride=rows), :]
        state = incoming_ref[lax.rem(code_ref[i], CODE)]
        product = jnp.dot(split_rows(mine), state, preferred_element_type=jnp.float32)
        moved_ref[pl.ds(row, STEPS, stride=room), :] = product[:STEPS] + product[STEPS:]
    for t in range(STEPS):
        here = slice(t * rows, (t + 1) * rows)
        readout = partial_ref[here] + moved_ref[t * room : t * room + rows]
        norm = lax.rsqrt(jnp.mean(readout * readout, axis=-1, keepdims=True) + 1e-05)
        normed = (readout * norm * gains_ref[here]).astype(jnp.bfloat16)
        for i in range(normed_ref.shape[0]):
            normed_ref[i, here] = normed


def output_kernel(ring_ref, *refs):
    weights, out_ref = refs[:XS], refs[XS]
    x = x_here()
    sources = [lax.rem(x + XS - k, XS) * CORES for k in range(XS)]
    rows = [
        jnp.concatenate([ring_ref[source + c] for c in range(CORES)], axis=1) for source in sources
    ]
    for z in range(ZS):
        total = 0.0
        for k in range(XS):
            total = total + jnp.dot(rows[k], weights[k][z], preferred_element_type=jnp.float32)
        out_ref[z] = total.astype(jnp.bfloat16)


def body(
    step_inputs,
    qkv_weight,
    out_weight,
    head_gain,
    head_decay,
    states_in,
    remaining_steps,
    migration_plan,
):
    rows = states_in.shape[0]
    count = STEPS * rows
    groups = lax.axis_size("group")
    own_group = lax.axis_index("group")
    states = states_in.reshape(rows, SIZE, SIZE)
    bf16, f32 = jnp.bfloat16, jnp.float32

    outgoing, inputs = pl.pallas_call(
        functools.partial(pack_kernel, rows),
        out_shape=[
            jax.ShapeDtypeStruct((groups * SLOTS, SIZE, SIZE), bf16),
            jax.ShapeDtypeStruct((count, SIZE), bf16),
        ],
        in_specs=[ANY, ANY, ANY],
        out_specs=[ANY, ANY],
        scratch_shapes=[
            pltpu.VMEM((ZH, YS * rows), jnp.int32),
            pltpu.VMEM((rows, SIZE, SIZE), f32),
            pltpu.VMEM((count, SIZE), bf16),
            pltpu.VMEM((MOVED, SIZE, SIZE), bf16),
            pltpu.SMEM((ZH * YS,), jnp.int32),
            DMA((3,)),
            DMA((MOVED + 1,)),
        ],
        compiler_params=ROOMY,
        name="pack",
    )(migration_plan.reshape(ZH, YS * rows), states, step_inputs.reshape(count, SIZE))
    passing = lax.all_to_all(outgoing, "group", 0, 0, tiled=True, axis_index_groups=Y_RINGS)
    line = lax.all_gather(inputs, "tensor", axis=0, axis_index_groups=Z_LINES)
    passing = pl.pallas_call(
        pass_kernel,
        out_shape=jax.ShapeDtypeStruct((ZH * PASSING, SIZE, SIZE), bf16),
        in_specs=[SMEM, VMEM, VMEM],
        out_specs=ANY,
        scratch_shapes=[pltpu.VMEM((ZH * PASSING, SIZE, SIZE), bf16), DMA((ZH,))],
        compiler_params=SMALL,
        name="pass_on",
    )(rows_on(migration_plan, own_group, groups, rows), passing, line)
    incoming = lax.all_to_all(passing, "group", 0, 0, tiled=True, axis_index_groups=Z_RINGS)

    plane = lax.all_gather(after(line, passing), "tensor", axis=0, axis_index_groups=X_RINGS)
    plane = plane.reshape(CHIPS, count, SIZE)
    other = lax.ppermute(plane, "tensor", CORE_SWAP)
    scaled, partial, gains, code = pl.pallas_call(
        functools.partial(project_kernel, rows),
        out_shape=[
            jax.ShapeDtypeStruct((count, SIZE), f32),
            jax.ShapeDtypeStruct((count, SIZE), f32),
            jax.ShapeDtypeStruct((count, SIZE), f32),
            jax.ShapeDtypeStruct((MOVED + 1,), jnp.int32),
        ],
        in_specs=[SMEM, SMEM, SMEM, VMEM, VMEM, VMEM, VMEM, VMEM],
        out_specs=[VMEM, VMEM, VMEM, SMEM],
        scratch_shapes=[
            pltpu.VMEM((count, SIZE), f32),
            pltpu.VMEM((count, SIZE), f32),
            pltpu.VMEM((rows, SIZE), jnp.int32),
            pltpu.SMEM((ZH,), jnp.int32),
        ],
        compiler_params=pltpu.CompilerParams(vmem_limit_bytes=16 * 2**20),
        cost_estimate=pl.CostEstimate(
            flops=2 * count * 4096 * 384, bytes_accessed=6 * 2**20, transcendentals=0
        ),
        name="project",
    )(
        migration_plan, remaining_steps, head_decay, head_gain.reshape(1, SIZE), plane, other,
        jnp.transpose(qkv_weight, (1, 0, 2)), states,
    )

    lent = pl.pallas_call(
        lend_kernel,
        out_shape=jax.ShapeDtypeStruct((XS, ZS, SIZE, SIZE), bf16),
        in_specs=[VMEM, ANY],
        out_specs=VMEM,
        compiler_params=SMALL,
        name="lend",
    )(out_weight, passing)
    lent = lax.ppermute(lent, "tensor", CORE_SWAP)
    dealt = pl.pallas_call(
        deal_kernel,
        out_shape=[jax.ShapeDtypeStruct((ZS, CORES * SIZE, SIZE), bf16)] * XS,
        in_specs=[VMEM, VMEM],
        out_specs=[VMEM] * XS,
        compiler_params=SMALL,
        name="deal",
    )(out_weight, lent)
    dealt = [dealt[0]] + [lax.ppermute(dealt[k], "tensor", X_SHIFTS[k]) for k in range(1, XS)]

    normed = pl.pallas_call(
        functools.partial(finish_kernel, rows),
        out_shape=jax.ShapeDtypeStruct((XS * CORES, count, SIZE), bf16),
        in_specs=[SMEM, VMEM, VMEM, VMEM, VMEM],
        out_specs=VMEM,
        scratch_shapes=[pltpu.VMEM((STEPS * (rows + 8), SIZE), f32)],
        compiler_params=SMALL,
        name="finish",
    )(code, scaled, partial, gains, incoming)
    ring = lax.all_to_all(normed, "tensor", 0, 0, tiled=True, axis_index_groups=X_CORES)
    sums = pl.pallas_call(
        output_kernel,
        out_shape=jax.ShapeDtypeStruct((ZS, count, SIZE), bf16),
        in_specs=[VMEM] * (1 + XS),
        out_specs=VMEM,
        compiler_params=SMALL,
        name="output",
    )(ring, *dealt)
    pieces = lax.all_to_all(sums, "tensor", 0, 0, tiled=True, axis_index_groups=Z_LINES)
    result = jnp.sum(pieces.astype(f32), axis=0).astype(bf16)
    return result.reshape(STEPS, rows, SIZE)


def solution(mesh):
    placed = (
        P(None, "group", "tensor"),
        P(None, None, "tensor"),
        P("tensor", None),
        P("tensor"),
        P("tensor"),
        P("group", "tensor", None, None),
        P(),
        P(),
    )
    return jax.shard_map(
        body, mesh=mesh, in_specs=placed, out_specs=P(None, "group", "tensor"), check_vma=False
    )
```
